32 devices in a mesh: blk: 4 (over y, x), regroup: 4 (over z), hid: 2 (over core).
Axes of the slice: x: 2, y: 2, z: 4, core: 2. Of those that a mesh axis runs over, the one named last changes fastest.
Arguments:
- tokens: bfloat16 [256, 6144], P(('blk', 'regroup')), may hold values from -6 to 6
- kinds: int32 [256], P(('blk', 'regroup')), may hold values from 0 to 7
- slots: int32 [16, 16], P(('blk', 'regroup')), may hold values from 0 to 15, each once within a row
- gains: float32 [8, 6144], replicated, may hold values from 0.1 to 1.9
- gate_weight: bfloat16 [6144, 16384], P(None, ('blk', 'hid')), may hold values from -0.078125 to 0.078125
- up_weight: bfloat16 [6144, 16384], P(None, ('blk', 'hid')), may hold values from -0.078125 to 0.078125
- down_weight: bfloat16 [16384, 6144], P(('blk', 'hid')), may hold values from -0.0625 to 0.0625
Outputs:
- mixed: bfloat16 [256, 6144], P(('blk', 'regroup'), 'hid')
The draws below stay inside these ranges and needn't reach their ends.
Inputs may be any that keep to these rules, and one draw needn't show every extreme that they name: Each row of slots names every number 0 to 15 once.
All inputs are finite; a program needn't handle non-finite values.
Results may differ from the reference program's by a relative error of at most 0.019.
Values may be sent and summed in bfloat16 or wider, within the bound.
No kernel may reach another device: no remote copies, remote signals or barrier semaphores. Data moves between devices by JAX's collectives and lax.ppermute only.
A program may use at most 128 MiB of HBM per device.

```python
import jax
import jax.numpy as jnp
from jax import lax

D = 6144
FF = 16384
KINDS = 8
PAT_DEV = 16
BLOCKS = 4
LANES = 4
ROUNDS = 4
TOKENS = 256
SHARDS = 8
SHARD_FF = 2048


def plant(values, stream_key, smallest, high):
    shape = values.shape
    place = [jax.random.randint(jax.random.fold_in(stream_key, axis), (), 0, shape[axis]) for axis in range(len(shape))]
    values = values.at[tuple(place)].set(smallest)
    longest = shape.index(max(shape))
    place[longest] = (place[longest] + 1) % shape[longest]
    return values.at[tuple(place)].set(high)


def with_spikes(entries, rng, source, target, shards_of, factor):
    def block_of(dim):
        return (jnp.arange(entries.shape[dim]) // (entries.shape[dim] // shards_of)).reshape((-1,) + (1,) * (entries.ndim - 1 - dim))

    near = jax.random.permutation(rng, shards_of)[block_of(target)]
    far = (block_of(target) + shards_of // 2) % shards_of
    return jnp.where((block_of(source) == near) | (block_of(source) == far), factor * entries, entries)


def block_scale(own_key, extent, split, low, high):
    factor_of, own = 1.0, jax.random.fold_in(own_key, 6)
    for axis_at, shards_of in split:
        heights = jnp.exp(jax.random.uniform(jax.random.fold_in(own, axis_at), (shards_of,), jnp.float32, low / len(split), high / len(split)))
        factor_of = factor_of * jnp.repeat(heights, extent[axis_at] // shards_of).reshape([-1 if axis == axis_at else 1 for axis in range(len(extent))])
    return factor_of


def gaussian(own_key, shape, spread, bound, cuts=(), held_as=jnp.bfloat16):
    factor_of = block_scale(own_key, shape, cuts, -0.22, 0.18) if cuts else 1.0
    array = jax.random.normal(own_key, shape, jnp.float32) * spread * factor_of
    return jnp.minimum(jnp.maximum(array, -bound), bound).astype(held_as)


def bell_draw_with(own_key, dims, deviation, most, split, heavy, dtype=jnp.bfloat16):
    array = deviation * jax.random.normal(own_key, dims, jnp.float32)
    if split:
        array = array * block_scale(own_key, dims, split, -0.22, 0.18)
    return jnp.clip(with_spikes(array, jax.random.fold_in(own_key, 3), *heavy), -most, most).astype(dtype)


def setup_inputs(seed: int = 0) -> dict:
    key_of = jax.random.split(jax.random.key(seed), 8)
    return {
        "tokens": gaussian(key_of[0], (TOKENS, D), 1.0, 6.0, ((0, 16),)),
        "kinds": plant(jax.random.randint(key_of[1], (TOKENS,), 0, KINDS), jax.random.fold_in(key_of[1], 1), 0, KINDS - 1).astype(jnp.int32),
        "slots": jax.vmap(lambda own: jax.random.permutation(own, PAT_DEV))(jax.random.split(key_of[2], (BLOCKS * LANES))).reshape((BLOCKS * LANES, PAT_DEV)).astype(jnp.int32),
        "gains": jnp.clip(1.0 + 0.18 * jax.random.normal(key_of[3], (KINDS, D), jnp.float32), 0.1, 1.9),
        "gate_weight": gaussian(key_of[4], (D, FF), D ** -0.5, 0.078125, ((1, 8),)),
        "up_weight": gaussian(key_of[5], (D, FF), D ** -0.5, 0.078125, ((1, 8),)),
        "down_weight": bell_draw_with(key_of[6], (FF, D), FF ** -0.5, 0.0625, ((0, 8),), (0, 1, 8, 2.0)),
    }


epsilon = 1e-05

def reference(tokens, kinds, slots, gains, gate_weight, up_weight, down_weight):
    width = tokens.shape[1]
    float_rows = tokens.astype(jnp.float32)
    row_scale = lax.rsqrt(lax.optimization_barrier(jnp.mean(float_rows * float_rows, axis=1, keepdims=True)) + epsilon)
    normed = (float_rows * row_scale * gains[kinds]).astype(jnp.bfloat16)
    grouped = normed.reshape(BLOCKS * LANES, PAT_DEV, width)
    inverse = jnp.argsort(slots, axis=1).astype(jnp.int32)
    ordered = jnp.take_along_axis(grouped, inverse[:, :, None], axis=1)
    arranged = ordered.reshape(BLOCKS, LANES, ROUNDS, LANES, width)
    arranged = jnp.transpose(arranged, (0, 3, 2, 1, 4)).reshape(TOKENS, width)
    gate_full = jnp.dot(arranged, gate_weight, preferred_element_type=jnp.float32)
    up_full = jnp.dot(arranged, up_weight, preferred_element_type=jnp.float32)
    hidden = (jax.nn.silu(gate_full) * up_full).astype(jnp.bfloat16)
    hidden_shards = jnp.transpose(hidden.reshape(TOKENS, SHARDS, SHARD_FF), (1, 0, 2))
    down_shards = down_weight.reshape(SHARDS, SHARD_FF, width)

    def add_term(summed, operands):
        rounded = jnp.dot(operands[0], operands[1], preferred_element_type=jnp.float32).astype(jnp.bfloat16)
        rounded = lax.optimization_barrier(rounded)
        return (summed + rounded.astype(jnp.float32), None)
    summed, unused = lax.scan(add_term, jnp.zeros((TOKENS, width), jnp.float32), (hidden_shards, down_shards))
    return summed.astype(jnp.bfloat16)
```

```python
import functools

import jax
import jax.numpy as jnp
from jax import lax
from jax.experimental import pallas as pl
from jax.experimental.pallas import tpu as pltpu
from jax.sharding import PartitionSpec as P

epsilon = 1e-05
MIB = 1 << 20

IN_HBM = pl.BlockSpec(memory_space=pltpu.HBM)
ANYWHERE = pl.BlockSpec(memory_space=pl.ANY)
IN_VMEM = pl.BlockSpec(memory_space=pltpu.VMEM)
IN_SMEM = pl.BlockSpec(memory_space=pltpu.SMEM)


def log2(number):
    bits = number.bit_length() - 1
    assert 1 << bits == number
    return bits


def exchange(array, axis, step):
    count = lax.axis_size(axis)
    log2(count)
    return lax.ppermute(array, axis, [(i, i ^ step) for i in range(count)])


def norm_kernel(lanes, tokens_ref, kinds_ref, slots_ref, gains_ref, out_ref):
    rows = tokens_ref.shape[0]
    rounds = rows // lanes
    x = tokens_ref[...].astype(jnp.float32)
    row_scale = lax.rsqrt(jnp.mean(x * x, axis=1, keepdims=True) + epsilon)
    at = lax.broadcasted_iota(jnp.int32, (rows, 1), 0)
    kind = jnp.zeros((rows, 1), jnp.int32)
    for i in range(rows):
        kind = jnp.where(at == i, kinds_ref[i], kind)
    gain = jnp.broadcast_to(gains_ref[0:1, :], x.shape)
    for c in range(1, gains_ref.shape[0]):
        gain = jnp.where(kind == c, gains_ref[c : c + 1, :], gain)
    normed = (x * row_scale * gain).astype(jnp.bfloat16)
    me = lax.axis_index("regroup")
    target = lax.broadcasted_iota(jnp.int32, (rows, rows), 0)
    lane = jnp.bitwise_xor(lax.shift_right_logical(target, log2(rounds)), me)
    slot = jnp.bitwise_and(target, rounds - 1) * lanes + lane
    placing = (jnp.broadcast_to(slots_ref[0:1, :], slot.shape) == slot).astype(jnp.bfloat16)
    out_ref[...] = jnp.dot(placing, normed, preferred_element_type=jnp.float32).astype(jnp.bfloat16)


def norm(tokens, kinds, slots, gains):
    return pl.pallas_call(
        functools.partial(norm_kernel, lax.axis_size("regroup")),
        out_shape=jax.ShapeDtypeStruct(tokens.shape, jnp.bfloat16),
        in_specs=[IN_VMEM, IN_SMEM, IN_VMEM, IN_VMEM],
        out_specs=IN_VMEM,
        compiler_params=pltpu.CompilerParams(vmem_limit_bytes=8 * MIB),
        name="norm",
    )(tokens, kinds, slots, gains)


def early_kernel(gate_ref, up_ref, gate_out, up_out, sems):
    width = gate_out.shape[1]
    copies = [
        pltpu.make_async_copy(src.at[:, pl.ds(0, width)], dst, sems.at[i])
        for i, (src, dst) in enumerate(((gate_ref, gate_out), (up_ref, up_out)))
    ]
    for copy in copies:
        copy.start()
    for copy in copies:
        copy.wait()


def early(gate_weight, up_weight, width):
    depth = gate_weight.shape[0]
    held = pltpu.VMEM((depth, width), jnp.bfloat16)
    return pl.pallas_call(
        early_kernel,
        out_shape=(held, held),
        in_specs=[IN_HBM, IN_HBM],
        out_specs=(IN_VMEM, IN_VMEM),
        scratch_shapes=[pltpu.SemaphoreType.DMA((2,))],
        compiler_params=pltpu.CompilerParams(vmem_limit_bytes=1 * MIB),
        cost_estimate=pl.CostEstimate(
            flops=0, bytes_accessed=8 * depth * width, transcendentals=0
        ),
        name="early",
    )(gate_weight, up_weight)


def by_steps(rows, blocks, lanes):
    rounds = rows // (blocks * lanes)
    r = lax.broadcasted_iota(jnp.int32, (rows, rows), 0)
    c = lax.broadcasted_iota(jnp.int32, (rows, rows), 1)
    m = jnp.bitwise_and(r, rounds - 1)
    rest = lax.shift_right_logical(r, log2(rounds))
    block = jnp.bitwise_and(rest, blocks - 1)
    lane = lax.shift_right_logical(rest, log2(blocks))
    return (c == (block * lanes + lane) * rounds + m).astype(jnp.bfloat16)


def by_place(rows, blocks, lanes, me):
    rounds = rows // (blocks * lanes)
    r = lax.broadcasted_iota(jnp.int32, (rows, rows), 0)
    c = lax.broadcasted_iota(jnp.int32, (rows, rows), 1)
    step = jnp.bitwise_xor(jnp.bitwise_and(r, lanes - 1), me)
    rest = lax.shift_right_logical(r, log2(lanes))
    m = jnp.bitwise_and(rest, rounds - 1)
    block = lax.shift_right_logical(rest, log2(rounds))
    return (c == (step * blocks + block) * rounds + m).astype(jnp.bfloat16)


def hidden_kernel(blocks, lanes, chunk, held_chunks, parts, slots, *refs):
    panel_refs = refs[:blocks]
    gate_held, up_held, gate_ref, up_ref = refs[blocks : blocks + 4]
    out_refs = refs[blocks + 4 : blocks + 4 + lanes]
    panel, gate_sum, up_sum, ring, sems = refs[blocks + 4 + lanes :]
    rows, depth = panel.shape
    part = depth // parts
    each = rows // blocks
    chunks = gate_ref.shape[1] // chunk
    units = [(c, p) for c in range(held_chunks, chunks) for p in range(parts)]

    def copies(n):
        c, p = units[n]
        return [
            pltpu.make_async_copy(
                src.at[pl.ds(p * part, part), pl.ds(c * chunk, chunk)],
                ring.at[n % slots, i],
                sems.at[n % slots, i],
            )
            for i, src in enumerate((gate_ref, up_ref))
        ]

    for n in range(min(slots, len(units))):
        for copy in copies(n):
            copy.start()
    for step, ref in enumerate(panel_refs):
        panel[step * each : (step + 1) * each, :] = ref[...]
    order = by_steps(rows, blocks, lanes)

    def finish(c, gate, up):
        hidden = (gate / (1.0 + jnp.exp(-gate)) * up).astype(jnp.bfloat16)
        placed = jnp.dot(order, hidden, preferred_element_type=jnp.float32).astype(jnp.bfloat16)
        span = rows // lanes
        for lane, ref in enumerate(out_refs):
            ref[:, c * chunk : (c + 1) * chunk] = placed[lane * span : (lane + 1) * span, :]

    for c in range(held_chunks):
        columns = slice(c * chunk, (c + 1) * chunk)
        x = panel[...]
        gate = jnp.dot(x, gate_held[:, columns], preferred_element_type=jnp.float32)
        up = jnp.dot(x, up_held[:, columns], preferred_element_type=jnp.float32)
        finish(c, gate, up)
    for n, (c, p) in enumerate(units):
        for copy in copies(n):
            copy.wait()
        x = panel[:, p * part : (p + 1) * part]
        gate = jnp.dot(x, ring[n % slots, 0], preferred_element_type=jnp.float32)
        up = jnp.dot(x, ring[n % slots, 1], preferred_element_type=jnp.float32)
        if n + slots < len(units):
            for copy in copies(n + slots):
                copy.start()
        if p > 0:
            gate += gate_sum[...]
            up += up_sum[...]
        if p < parts - 1:
            gate_sum[...] = gate
            up_sum[...] = up
        else:
            finish(c, gate, up)


def hidden_part(panels, gate_held, up_held, gate_weight, up_weight, chunk, parts, slots):
    blocks, lanes = len(panels), lax.axis_size("regroup")
    each, depth = panels[0].shape
    rows = blocks * each
    width = gate_weight.shape[1]
    piece = jax.ShapeDtypeStruct((rows // lanes, width), jnp.bfloat16)
    return pl.pallas_call(
        functools.partial(
            hidden_kernel, blocks, lanes, chunk, gate_held.shape[1] // chunk, parts, slots
        ),
        out_shape=(piece,) * lanes,
        in_specs=[IN_VMEM] * blocks + [IN_VMEM, IN_VMEM, IN_HBM, IN_HBM],
        out_specs=(IN_VMEM,) * lanes,
        scratch_shapes=[
            pltpu.VMEM((rows, depth), jnp.bfloat16),
            pltpu.VMEM((rows, chunk), jnp.float32),
            pltpu.VMEM((rows, chunk), jnp.float32),
            pltpu.VMEM((slots, 2, depth // parts, chunk), jnp.bfloat16),
            pltpu.SemaphoreType.DMA((slots, 2)),
        ],
        compiler_params=pltpu.CompilerParams(vmem_limit_bytes=18 * MIB),
        cost_estimate=pl.CostEstimate(
            flops=4 * rows * depth * width,
            bytes_accessed=4 * depth * width,
            transcendentals=rows * width,
        ),
        name="hidden_part",
    )(*panels, gate_held, up_held, gate_weight, up_weight)


def down_kernel(blocks, lanes, chunk, *refs):
    piece_refs = refs[:lanes]
    down_ref = refs[lanes]
    out_refs = refs[lanes + 1 : -2]
    stack, hidden = refs[-2:]
    rows = hidden.shape[0]
    span = rows // lanes
    for step, ref in enumerate(piece_refs):
        stack[step * span : (step + 1) * span, :] = ref[...]
    order = by_place(rows, blocks, lanes, lax.axis_index("regroup"))
    hidden[...] = jnp.dot(order, stack[...], preferred_element_type=jnp.float32).astype(
        jnp.bfloat16
    )
    me = lax.axis_index("hid")
    for step in reversed(range(len(out_refs))):
        width = out_refs[step].shape[1]
        start = jnp.bitwise_xor(me, step) * width
        for c in range(width // chunk):
            at = pl.multiple_of(start + c * chunk, chunk)
            out_refs[step][:, c * chunk : (c + 1) * chunk] = jnp.dot(
                hidden[...], down_ref[:, pl.ds(at, chunk)], preferred_element_type=jnp.float32
            ).astype(out_refs[step].dtype)


def down_part(pieces, down_weight, blocks, chunk):
    lanes, hids = len(pieces), lax.axis_size("hid")
    rows = lanes * pieces[0].shape[0]
    depth, features = down_weight.shape
    width = features // hids
    outs = [jax.ShapeDtypeStruct((rows, width), jnp.float32)]
    outs += [jax.ShapeDtypeStruct((rows, width), jnp.bfloat16)] * (hids - 1)
    return pl.pallas_call(
        functools.partial(down_kernel, blocks, lanes, chunk),
        out_shape=tuple(outs),
        in_specs=[IN_VMEM] * (lanes + 1),
        out_specs=(IN_VMEM,) * hids,
        scratch_shapes=[
            pltpu.VMEM((rows, depth), jnp.bfloat16),
            pltpu.VMEM((rows, depth), jnp.bfloat16),
        ],
        compiler_params=pltpu.CompilerParams(vmem_limit_bytes=30 * MIB),
        cost_estimate=pl.CostEstimate(
            flops=2 * rows * depth * features,
            bytes_accessed=2 * depth * features,
            transcendentals=0,
        ),
        name="down_part",
    )(*pieces, down_weight)


def hid_sum_kernel(count, *refs):
    total = refs[0][...]
    for ref in refs[1:count]:
        total += ref[...].astype(jnp.float32)
    each = total.shape[0] // len(refs[count:])
    for step, ref in enumerate(refs[count:]):
        ref[...] = total[step * each : (step + 1) * each, :].astype(ref.dtype)


def hid_sum(parts, blocks):
    rows, width = parts[0].shape
    each = rows // blocks
    outs = [jax.ShapeDtypeStruct((each, width), jnp.float32)]
    outs += [jax.ShapeDtypeStruct((each, width), jnp.bfloat16)] * (blocks - 1)
    return pl.pallas_call(
        functools.partial(hid_sum_kernel, len(parts)),
        out_shape=tuple(outs),
        in_specs=[IN_VMEM] * len(parts),
        out_specs=(IN_VMEM,) * blocks,
        compiler_params=pltpu.CompilerParams(vmem_limit_bytes=8 * MIB),
        name="hid_sum",
    )(*parts)


def blk_sum_kernel(*refs):
    total = refs[0][...]
    for ref in refs[1:-1]:
        total += ref[...].astype(jnp.float32)
    refs[-1][...] = total.astype(refs[-1].dtype)


def blk_sum(parts):
    return pl.pallas_call(
        blk_sum_kernel,
        out_shape=jax.ShapeDtypeStruct(parts[0].shape, jnp.bfloat16),
        in_specs=[IN_VMEM] * len(parts),
        out_specs=IN_VMEM,
        compiler_params=pltpu.CompilerParams(vmem_limit_bytes=8 * MIB),
        name="blk_sum",
    )(*parts)


def on_device(tokens, kinds, slots, gains, gate_weight, up_weight, down_weight):
    blocks, lanes, hids = (lax.axis_size(axis) for axis in ("blk", "regroup", "hid"))
    shard = gate_weight.shape[1]
    chunk = min(512, shard)
    rows = norm(tokens, kinds, slots, gains)
    panels = [rows] + [exchange(rows, "blk", step) for step in range(1, blocks)]
    gate_held, up_held = early(gate_weight, up_weight, chunk)
    pieces = hidden_part(panels, gate_held, up_held, gate_weight, up_weight, chunk, 4, 4)
    pieces = [pieces[0]] + [
        exchange(pieces[step], "regroup", step) for step in range(1, lanes)
    ]
    partial = down_part(pieces, down_weight, blocks, min(512, down_weight.shape[1] // hids))
    partial = [partial[0]] + [exchange(partial[step], "hid", step) for step in range(1, hids)]
    own = hid_sum(partial, blocks)
    return blk_sum([own[0]] + [exchange(own[step], "blk", step) for step in range(1, blocks)])


def solution(mesh):
    placed = (
        P(("blk", "regroup"), None),
        P(("blk", "regroup")),
        P(("blk", "regroup"), None),
        P(),
        P(None, ("blk", "hid")),
        P(None, ("blk", "hid")),
        P(("blk", "hid"), None),
    )
    return jax.shard_map(
        on_device,
        mesh=mesh,
        in_specs=placed,
        out_specs=P(("blk", "regroup"), "hid"),
        check_vma=False,
    )
```

```python
import functools

import jax
import jax.numpy as jnp
from jax import lax
from jax.experimental import pallas as pl
from jax.experimental.pallas import tpu as pltpu
from jax.sharding import PartitionSpec as P

epsilon = 1e-05
MIB = 1 << 20

ANYWHERE = pl.BlockSpec(memory_space=pl.ANY)
IN_VMEM = pl.BlockSpec(memory_space=pltpu.VMEM)


def log2(number):
    bits = number.bit_length() - 1
    assert 1 << bits == number
    return bits


def exchange(array, axis, step):
    count = lax.axis_size(axis)
    log2(count)
    return lax.ppermute(array, axis, [(i, i ^ step) for i in range(count)])


def norm_kernel(lanes, *refs):
    sources, piece_refs = refs[:4], refs[4 : 4 + lanes]
    targets, placed, sems = refs[4 + lanes : 8 + lanes], refs[8 + lanes], refs[9 + lanes]
    copies = [
        pltpu.make_async_copy(src, dst, sems.at[i])
        for i, (src, dst) in enumerate(zip(sources, targets))
    ]
    for copy in copies:
        copy.start()
    for copy in copies:
        copy.wait()
    tokens_ref, kinds_ref, slots_ref, gains_ref = targets
    rows = tokens_ref.shape[0]
    rounds = rows // lanes
    x = tokens_ref[...].astype(jnp.float32)
    row_scale = lax.rsqrt(jnp.mean(x * x, axis=1, keepdims=True) + epsilon)
    width = placed.shape[1]
    columns = pl.ds(pl.multiple_of(lax.axis_index("hid") * width, width), width)
    x = tokens_ref[:, columns].astype(jnp.float32)
    at = lax.broadcasted_iota(jnp.int32, (rows, 1), 0)
    kind = jnp.zeros((rows, 1), jnp.int32)
    for i in range(rows):
        kind = jnp.where(at == i, kinds_ref[i], kind)
    gain = jnp.broadcast_to(gains_ref[0:1, columns], x.shape)
    for c in range(1, gains_ref.shape[0]):
        gain = jnp.where(kind == c, gains_ref[c : c + 1, columns], gain)
    normed = (x * row_scale * gain).astype(jnp.bfloat16)
    me = lax.axis_index("regroup")
    target = lax.broadcasted_iota(jnp.int32, (rows, rows), 0)
    lane = jnp.bitwise_xor(lax.shift_right_logical(target, log2(rounds)), me)
    slot = jnp.bitwise_and(target, rounds - 1) * lanes + lane
    placing = (jnp.broadcast_to(slots_ref[0:1, :], slot.shape) == slot).astype(jnp.bfloat16)
    placed[...] = jnp.dot(placing, normed, preferred_element_type=jnp.float32)
    for step, ref in enumerate(piece_refs):
        ref[...] = placed[step * rounds : (step + 1) * rounds, :].astype(jnp.bfloat16)


def norm(tokens, kinds, slots, gains):
    rows, features = tokens.shape
    lanes = lax.axis_size("regroup")
    width = features // lax.axis_size("hid")
    return pl.pallas_call(
        functools.partial(norm_kernel, lanes),
        out_shape=(jax.ShapeDtypeStruct((rows // lanes, width), jnp.bfloat16),) * lanes,
        in_specs=[ANYWHERE] * 4,
        out_specs=(IN_VMEM,) * lanes,
        scratch_shapes=[
            pltpu.VMEM(tokens.shape, tokens.dtype),
            pltpu.SMEM(kinds.shape, kinds.dtype),
            pltpu.VMEM(slots.shape, slots.dtype),
            pltpu.VMEM(gains.shape, gains.dtype),
            pltpu.VMEM((rows, width), jnp.float32),
            pltpu.SemaphoreType.DMA((4,)),
        ],
        compiler_params=pltpu.CompilerParams(vmem_limit_bytes=4 * MIB),
        cost_estimate=pl.CostEstimate(flops=0, bytes_accessed=48 * MIB, transcendentals=0),
        name="norm",
    )(tokens, kinds, slots, gains)


def arrange_kernel(lanes, *refs):
    out_ref, stack = refs[lanes:]
    rows = out_ref.shape[0]
    rounds = rows // lanes
    for step in range(lanes):
        stack[step * rounds : (step + 1) * rounds, :] = refs[step][...].astype(jnp.float32)
    r = lax.broadcasted_iota(jnp.int32, (rows, rows), 0)
    c = lax.broadcasted_iota(jnp.int32, (rows, rows), 1)
    step = jnp.bitwise_xor(jnp.bitwise_and(r, lanes - 1), lax.axis_index("regroup"))
    order = (c == step * rounds + lax.shift_right_logical(r, log2(lanes))).astype(jnp.bfloat16)
    out_ref[...] = jnp.dot(
        order, stack[...].astype(jnp.bfloat16), preferred_element_type=jnp.float32
    ).astype(jnp.bfloat16)


def arrange(pieces):
    lanes = len(pieces)
    rounds, width = pieces[0].shape
    return pl.pallas_call(
        functools.partial(arrange_kernel, lanes),
        out_shape=jax.ShapeDtypeStruct((lanes * rounds, width), jnp.bfloat16),
        in_specs=[IN_VMEM] * lanes,
        out_specs=IN_VMEM,
        scratch_shapes=[pltpu.VMEM((lanes * rounds, width), jnp.float32)],
        compiler_params=pltpu.CompilerParams(vmem_limit_bytes=4 * MIB),
        name="arrange",
    )(*pieces)


def early_kernel(after_ref, up_ref, out_ref, sem):
    depth = out_ref.shape[0]
    start = pl.multiple_of(lax.axis_index("hid") * depth, depth)
    copy = pltpu.make_async_copy(up_ref.at[pl.ds(start, depth), :], out_ref, sem)
    copy.start()
    copy.wait()


def early(after, up_weight):
    depth = up_weight.shape[0] // lax.axis_size("hid")
    shard = up_weight.shape[1]
    return pl.pallas_call(
        early_kernel,
        out_shape=pltpu.VMEM((depth, shard), jnp.bfloat16),
        in_specs=[ANYWHERE, ANYWHERE],
        out_specs=IN_VMEM,
        scratch_shapes=[pltpu.SemaphoreType.DMA(())],
        compiler_params=pltpu.CompilerParams(vmem_limit_bytes=1 * MIB),
        cost_estimate=pl.CostEstimate(
            flops=0, bytes_accessed=2 * depth * shard, transcendentals=0
        ),
        name="early",
    )(after, up_weight)


def even(total, most):
    return next(size for size in range(min(most, total), 0, -128) if total % size == 0)


def ffn_kernel(blocks, hids, plan, *refs):
    slots, part, up_cols, down_rows, down_cols = plan
    count = blocks * hids
    panel_refs = refs[:count]
    gate_ref, held_ref, up_ref, down_ref = refs[count : count + 4]
    hidden_ref, kept = refs[count + 4 : count + 6]
    out_refs = refs[count + 6 : count + 5 + hids]
    panel, up_sum, ring, ring_sems, kept_sem = refs[count + 5 + hids :]
    rows, depth = panel.shape
    each = rows // blocks
    shard = gate_ref.shape[1]
    width = depth // hids
    me = lax.axis_index("hid")
    inside, across = width // part, shard // up_cols
    deep, wide = shard // down_rows, width // down_cols
    up_count = (hids - 1) * inside * across
    down_count = (hids - 1) * wide * deep

    def side_start(side):
        return jnp.bitwise_xor(me, side) * width

    def up_copy(n):
        side, p, c = n // (inside * across) + 1, n // across % inside, n % across
        return pltpu.make_async_copy(
            up_ref.at[
                pl.ds(pl.multiple_of(side_start(side) + p * part, part), part),
                pl.ds(pl.multiple_of(c * up_cols, up_cols), up_cols),
            ],
            ring.at[n % slots, pl.ds(0, part), pl.ds(0, up_cols)],
            ring_sems.at[n % slots],
        )

    def down_copy(n):
        side, c, k = n // (wide * deep) + 1, n // deep % wide, n % deep
        slot = (n + up_count) % slots
        return pltpu.make_async_copy(
            down_ref.at[
                pl.ds(pl.multiple_of(k * down_rows, down_rows), down_rows),
                pl.ds(pl.multiple_of(side_start(side) + c * down_cols, 128), down_cols),
            ],
            ring.at[slot, pl.ds(0, down_rows), pl.ds(0, down_cols)],
            ring_sems.at[slot],
        )

    kept_copy = pltpu.make_async_copy(
        down_ref.at[:, pl.ds(pl.multiple_of(me * width, 128), kept.shape[1])], kept, kept_sem
    )

    def start_next(n):
        if isinstance(n, int):
            if n < up_count:
                up_copy(n).start()
            elif n < up_count + down_count:
                down_copy(n - up_count).start()
            return

        @pl.when(n < up_count)
        def _():
            up_copy(n).start()

        @pl.when((n >= up_count) & (n < up_count + down_count))
        def _():
            down_copy(n - up_count).start()

    for n in range(slots):
        start_next(n)
    for side in range(hids):
        start = pl.multiple_of(side_start(side), width)
        for step in range(blocks):
            panel[step * each : (step + 1) * each, pl.ds(start, width)] = panel_refs[
                side * blocks + step
            ][...]
    chunk = min(1024, shard)
    own = pl.ds(pl.multiple_of(me * width, width), width)

    @pl.loop(0, shard // chunk)
    def _(c):
        columns = pl.ds(pl.multiple_of(c * chunk, chunk), chunk)
        up_sum[:, columns] = jnp.dot(
            panel[:, own], held_ref[:, columns], preferred_element_type=jnp.float32
        )

    @pl.loop(0, (hids - 1) * inside)
    def _(u):
        side, p = u // inside + 1, u % inside
        x = panel[:, pl.ds(pl.multiple_of(side_start(side) + p * part, part), part)]
        for c in range(across):
            n = u * across + c
            up_copy(n).wait()
            columns = slice(c * up_cols, (c + 1) * up_cols)
            up_sum[:, columns] += jnp.dot(
                x,
                ring[n % slots, 0:part, 0:up_cols],
                preferred_element_type=jnp.float32,
            )
            start_next(n + slots)

    kept_copy.start()

    @pl.loop(0, shard // chunk)
    def _(c):
        columns = pl.ds(pl.multiple_of(c * chunk, chunk), chunk)
        gate = jnp.dot(panel[...], gate_ref[:, columns], preferred_element_type=jnp.float32)
        hidden_ref[:, columns] = (gate / (1.0 + jnp.exp(-gate)) * up_sum[:, columns]).astype(
            jnp.bfloat16
        )

    for side in range(1, hids):

        @pl.loop(0, wide)
        def _(c):
            total = None
            for k in range(deep):
                n = ((side - 1) * wide + c) * deep + k
                down_copy(n).wait()
                value = jnp.dot(
                    hidden_ref[:, k * down_rows : (k + 1) * down_rows],
                    ring[(n + up_count) % slots, 0:down_rows, 0:down_cols],
                    preferred_element_type=jnp.float32,
                )
                total = value if total is None else total + value
                start_next(n + up_count + slots)
            columns = pl.ds(pl.multiple_of(c * down_cols, 128), down_cols)
            out_refs[side - 1][:, columns] = total.astype(jnp.bfloat16)

    kept_copy.wait()


def ffn(panels, gate_weight, up_held, up_weight, down_weight, blocks):
    hids = lax.axis_size("hid")
    each, width = panels[0].shape
    rows, depth = blocks * each, width * hids
    shard = gate_weight.shape[1]
    part, up_cols = even(width, 1024), even(shard, 1024)
    down_rows, down_cols = even(shard, 1024), even(width, 1024)
    slots = 4
    outs = [
        pltpu.VMEM((rows, shard), jnp.bfloat16),
        pltpu.VMEM((shard, (width // down_cols + 1) // 2 * down_cols), jnp.bfloat16),
    ] + [pltpu.VMEM((rows, width), jnp.bfloat16)] * (hids - 1)
    return pl.pallas_call(
        functools.partial(
            ffn_kernel, blocks, hids, (slots, part, up_cols, down_rows, down_cols)
        ),
        out_shape=tuple(outs),
        in_specs=[IN_VMEM] * (len(panels) + 2) + [ANYWHERE, ANYWHERE],
        out_specs=(IN_VMEM,) * (1 + hids),
        scratch_shapes=[
            pltpu.VMEM((rows, depth), jnp.bfloat16),
            pltpu.VMEM((rows, shard), jnp.float32),
            pltpu.VMEM((slots, max(part, down_rows), max(up_cols, down_cols)), jnp.bfloat16),
            pltpu.SemaphoreType.DMA((slots,)),
            pltpu.SemaphoreType.DMA(()),
        ],
        compiler_params=pltpu.CompilerParams(vmem_limit_bytes=13 * MIB),
        cost_estimate=pl.CostEstimate(
            flops=4 * rows * depth * shard + 2 * rows * shard * (depth - width),
            bytes_accessed=4 * depth * shard,
            transcendentals=rows * shard,
        ),
        name="ffn",
    )(*panels, gate_weight, up_held, up_weight, down_weight)


def kept_kernel(hidden_ref, kept_ref, down_ref, out_ref, rest, sems):
    width = out_ref.shape[1]
    have, band = kept_ref.shape[1], rest.shape[2]
    me = lax.axis_index("hid")

    def copy(n):
        start = pl.multiple_of(me * width + have + n * band, 128)
        return pltpu.make_async_copy(
            down_ref.at[:, pl.ds(start, band)], rest.at[n], sems.at[n]
        )

    more = (width - have) // band
    for n in range(more):
        copy(n).start()

    @pl.loop(0, have // band)
    def _(n):
        columns = pl.ds(pl.multiple_of(n * band, 128), band)
        out_ref[:, columns] = jnp.dot(
            hidden_ref[...], kept_ref[:, columns], preferred_element_type=jnp.float32
        )

    @pl.loop(0, more)
    def _(n):
        copy(n).wait()
        columns = pl.ds(pl.multiple_of(have + n * band, 128), band)
        out_ref[:, columns] = jnp.dot(
            hidden_ref[...], rest[n], preferred_element_type=jnp.float32
        )


def kept_part(hidden, kept, down_weight):
    rows, shard = hidden.shape
    width = down_weight.shape[1] // lax.axis_size("hid")
    band = even(kept.shape[1], 512)
    more = max(1, (width - kept.shape[1]) // band)
    return pl.pallas_call(
        kept_kernel,
        out_shape=jax.ShapeDtypeStruct((rows, width), jnp.float32),
        in_specs=[IN_VMEM, IN_VMEM, ANYWHERE],
        out_specs=IN_VMEM,
        scratch_shapes=[
            pltpu.VMEM((more, shard, band), jnp.bfloat16),
            pltpu.SemaphoreType.DMA((more,)),
        ],
        compiler_params=pltpu.CompilerParams(vmem_limit_bytes=6 * MIB),
        cost_estimate=pl.CostEstimate(
            flops=2 * rows * shard * width, bytes_accessed=2 * shard * width, transcendentals=0
        ),
        name="kept_part",
    )(hidden, kept, down_weight)


def hid_sum_kernel(count, *refs):
    total = refs[0][...]
    for ref in refs[1:count]:
        total += ref[...].astype(jnp.float32)
    each = total.shape[0] // len(refs[count:])
    for step, ref in enumerate(refs[count:]):
        ref[...] = total[step * each : (step + 1) * each, :].astype(ref.dtype)


def hid_sum(parts, blocks):
    rows, width = parts[0].shape
    each = rows // blocks
    outs = [jax.ShapeDtypeStruct((each, width), jnp.float32)]
    outs += [jax.ShapeDtypeStruct((each, width), jnp.bfloat16)] * (blocks - 1)
    return pl.pallas_call(
        functools.partial(hid_sum_kernel, len(parts)),
        out_shape=tuple(outs),
        in_specs=[IN_VMEM] * len(parts),
        out_specs=(IN_VMEM,) * blocks,
        compiler_params=pltpu.CompilerParams(vmem_limit_bytes=4 * MIB),
        name="hid_sum",
    )(*parts)


def blk_sum_kernel(*refs):
    total = refs[0][...]
    for ref in refs[1:-1]:
        total += ref[...].astype(jnp.float32)
    refs[-1][...] = total.astype(refs[-1].dtype)


def blk_sum(parts):
    return pl.pallas_call(
        blk_sum_kernel,
        out_shape=jax.ShapeDtypeStruct(parts[0].shape, jnp.bfloat16),
        in_specs=[IN_VMEM] * len(parts),
        out_specs=IN_VMEM,
        compiler_params=pltpu.CompilerParams(vmem_limit_bytes=4 * MIB),
        name="blk_sum",
    )(*parts)


def held(array):
    return pltpu.with_memory_space_constraint(array, pltpu.VMEM)


def on_device(tokens, kinds, slots, gains, gate_weight, up_weight, down_weight):
    blocks, lanes, hids = (lax.axis_size(axis) for axis in ("blk", "regroup", "hid"))
    tokens, kinds, slots, gains, up_weight, down_weight = (
        pltpu.with_memory_space_constraint(array, pltpu.HBM)
        for array in (tokens, kinds, slots, gains, up_weight, down_weight)
    )
    gate_weight = held(gate_weight)
    pieces = norm(tokens, kinds, slots, gains)
    half = arrange(
        [pieces[0]] + [exchange(pieces[step], "regroup", step) for step in range(1, lanes)]
    )
    halves = [half] + [exchange(half, "blk", step) for step in range(1, blocks)]
    up_held = held(early(half, up_weight))
    halves, up_held = lax.optimization_barrier((halves, up_held))
    up_held = held(up_held)
    panels = halves + [exchange(part, "hid", side) for side in range(1, hids) for part in halves]
    panels = [held(part) for part in panels]
    hidden, kept, *sent = ffn(panels, gate_weight, up_held, up_weight, down_weight, blocks)
    hidden, kept = held(hidden), held(kept)
    came = [exchange(part, "hid", step + 1) for step, part in enumerate(sent)]
    parts = hid_sum([kept_part(hidden, kept, down_weight)] + came, blocks)
    return blk_sum(
        [parts[0]] + [exchange(parts[step], "blk", step) for step in range(1, blocks)]
    )


def solution(mesh):
    placed = (
        P(("blk", "regroup"), None),
        P(("blk", "regroup")),
        P(("blk", "regroup"), None),
        P(),
        P(None, ("blk", "hid")),
        P(None, ("blk", "hid")),
        P(("blk", "hid"), None),
    )
    return jax.shard_map(
        on_device,
        mesh=mesh,
        in_specs=placed,
        out_specs=P(("blk", "regroup"), "hid"),
        check_vma=False,
    )
```

```python
import functools

import jax
import jax.numpy as jnp
from jax import lax
from jax.experimental import pallas as pl
from jax.experimental.pallas import tpu as pltpu
from jax.sharding import PartitionSpec as P

epsilon = 1e-05
MIB = 1 << 20

ANYWHERE = pl.BlockSpec(memory_space=pl.ANY)
IN_VMEM = pl.BlockSpec(memory_space=pltpu.VMEM)


def log2(number):
    bits = number.bit_length() - 1
    assert 1 << bits == number
    return bits


def exchange(array, axis, step):
    count = lax.axis_size(axis)
    log2(count)
    return lax.ppermute(array, axis, [(i, i ^ step) for i in range(count)])


def norm_kernel(lanes, *refs):
    sources, piece_refs = refs[:4], refs[4 : 4 + lanes]
    targets, placed, sems = refs[4 + lanes : 8 + lanes], refs[8 + lanes], refs[9 + lanes]
    copies = [
        pltpu.make_async_copy(src, dst, sems.at[i])
        for i, (src, dst) in enumerate(zip(sources, targets))
    ]
    for copy in copies:
        copy.start()
    for copy in copies:
        copy.wait()
    tokens_ref, kinds_ref, slots_ref, gains_ref = targets
    rows = tokens_ref.shape[0]
    rounds = rows // lanes
    x = tokens_ref[...].astype(jnp.float32)
    row_scale = lax.rsqrt(jnp.mean(x * x, axis=1, keepdims=True) + epsilon)
    width = placed.shape[1]
    columns = pl.ds(pl.multiple_of(lax.axis_index("hid") * width, width), width)
    x = tokens_ref[:, columns].astype(jnp.float32)
    at = lax.broadcasted_iota(jnp.int32, (rows, 1), 0)
    kind = jnp.zeros((rows, 1), jnp.int32)
    for i in range(rows):
        kind = jnp.where(at == i, kinds_ref[i], kind)
    gain = jnp.broadcast_to(gains_ref[0:1, columns], x.shape)
    for c in range(1, gains_ref.shape[0]):
        gain = jnp.where(kind == c, gains_ref[c : c + 1, columns], gain)
    normed = (x * row_scale * gain).astype(jnp.bfloat16)
    me = lax.axis_index("regroup")
    target = lax.broadcasted_iota(jnp.int32, (rows, rows), 0)
    lane = jnp.bitwise_xor(lax.shift_right_logical(target, log2(rounds)), me)
    slot = jnp.bitwise_and(target, rounds - 1) * lanes + lane
    placing = (jnp.broadcast_to(slots_ref[0:1, :], slot.shape) == slot).astype(jnp.bfloat16)
    placed[...] = jnp.dot(placing, normed, preferred_element_type=jnp.float32)
    for step, ref in enumerate(piece_refs):
        ref[...] = placed[step * rounds : (step + 1) * rounds, :].astype(jnp.bfloat16)


def norm(tokens, kinds, slots, gains):
    rows, features = tokens.shape
    lanes = lax.axis_size("regroup")
    width = features // lax.axis_size("hid")
    return pl.pallas_call(
        functools.partial(norm_kernel, lanes),
        out_shape=(jax.ShapeDtypeStruct((rows // lanes, width), jnp.bfloat16),) * lanes,
        in_specs=[ANYWHERE] * 4,
        out_specs=(IN_VMEM,) * lanes,
        scratch_shapes=[
            pltpu.VMEM(tokens.shape, tokens.dtype),
            pltpu.SMEM(kinds.shape, kinds.dtype),
            pltpu.VMEM(slots.shape, slots.dtype),
            pltpu.VMEM(gains.shape, gains.dtype),
            pltpu.VMEM((rows, width), jnp.float32),
            pltpu.SemaphoreType.DMA((4,)),
        ],
        compiler_params=pltpu.CompilerParams(vmem_limit_bytes=4 * MIB),
        cost_estimate=pl.CostEstimate(flops=0, bytes_accessed=48 * MIB, transcendentals=0),
        name="norm",
    )(tokens, kinds, slots, gains)


def arrange_kernel(lanes, *refs):
    out_ref, stack = refs[lanes:]
    rows = out_ref.shape[0]
    rounds = rows // lanes
    for step in range(lanes):
        stack[step * rounds : (step + 1) * rounds, :] = refs[step][...].astype(jnp.float32)
    r = lax.broadcasted_iota(jnp.int32, (rows, rows), 0)
    c = lax.broadcasted_iota(jnp.int32, (rows, rows), 1)
    step = jnp.bitwise_xor(jnp.bitwise_and(r, lanes - 1), lax.axis_index("regroup"))
    order = (c == step * rounds + lax.shift_right_logical(r, log2(lanes))).astype(jnp.bfloat16)
    out_ref[...] = jnp.dot(
        order, stack[...].astype(jnp.bfloat16), preferred_element_type=jnp.float32
    ).astype(jnp.bfloat16)


def arrange(pieces):
    lanes = len(pieces)
    rounds, width = pieces[0].shape
    return pl.pallas_call(
        functools.partial(arrange_kernel, lanes),
        out_shape=jax.ShapeDtypeStruct((lanes * rounds, width), jnp.bfloat16),
        in_specs=[IN_VMEM] * lanes,
        out_specs=IN_VMEM,
        scratch_shapes=[pltpu.VMEM((lanes * rounds, width), jnp.float32)],
        compiler_params=pltpu.CompilerParams(vmem_limit_bytes=4 * MIB),
        name="arrange",
    )(*pieces)


def even(total, most):
    return next(size for size in range(min(most, total), 0, -128) if total % size == 0)


def early_kernel(width, after_ref, up_ref, out_ref, sem):
    start = pl.multiple_of(lax.axis_index("hid") * width, width)
    copy = pltpu.make_async_copy(up_ref.at[pl.ds(start, out_ref.shape[0]), :], out_ref, sem)
    copy.start()
    copy.wait()


def early(after, up_weight):
    width = up_weight.shape[0] // lax.axis_size("hid")
    depth = width - even(width, 1024)
    shard = up_weight.shape[1]
    return pl.pallas_call(
        functools.partial(early_kernel, width),
        out_shape=pltpu.VMEM((depth, shard), jnp.bfloat16),
        in_specs=[ANYWHERE, ANYWHERE],
        out_specs=IN_VMEM,
        scratch_shapes=[pltpu.SemaphoreType.DMA(())],
        compiler_params=pltpu.CompilerParams(vmem_limit_bytes=1 * MIB),
        cost_estimate=pl.CostEstimate(
            flops=0, bytes_accessed=2 * depth * shard, transcendentals=0
        ),
        name="early",
    )(after, up_weight)


def ffn_kernel(blocks, hids, plan, *refs):
    slots, part, up_cols, down_rows, down_cols = plan
    count = blocks * hids
    panel_refs = refs[:count]
    gate_ref, held_ref, up_ref, down_ref = refs[count : count + 4]
    hidden_ref, kept = refs[count + 4 : count + 6]
    out_refs = refs[count + 6 : count + 5 + hids]
    panel, up_sum, act, ring, ring_sems, kept_sems = refs[count + 5 + hids :]
    rows, depth = panel.shape
    each = rows // blocks
    shard = gate_ref.shape[1]
    width = depth // hids
    me = lax.axis_index("hid")
    inside, across = width // part, shard // up_cols
    deep, wide = shard // down_rows, width // down_cols
    skip = held_ref.shape[0] // part
    up_count = (hids * inside - skip) * across
    down_count = (hids - 1) * wide * deep

    def side_start(side):
        return jnp.bitwise_xor(me, side) * width

    def up_copy(n):
        u, c = n // across + skip, n % across
        side, p = u // inside, u % inside
        return pltpu.make_async_copy(
            up_ref.at[
                pl.ds(pl.multiple_of(side_start(side) + p * part, part), part),
                pl.ds(pl.multiple_of(c * up_cols, up_cols), up_cols),
            ],
            ring.at[n % slots, pl.ds(0, part), pl.ds(0, up_cols)],
            ring_sems.at[n % slots],
        )

    def down_copy(n):
        side, c, k = n // (wide * deep) + 1, n // deep % wide, n % deep
        slot = (n + up_count) % slots
        return pltpu.make_async_copy(
            down_ref.at[
                pl.ds(pl.multiple_of(k * down_rows, down_rows), down_rows),
                pl.ds(pl.multiple_of(side_start(side) + c * down_cols, 128), down_cols),
            ],
            ring.at[slot, pl.ds(0, down_rows), pl.ds(0, down_cols)],
            ring_sems.at[slot],
        )

    def kept_copy(n):
        size = kept.shape[1] // 2
        start = pl.multiple_of(me * width + n * size, 128)
        return pltpu.make_async_copy(
            down_ref.at[:, pl.ds(start, size)],
            kept.at[:, n * size : (n + 1) * size],
            kept_sems.at[n],
        )

    def start_next(n):
        if isinstance(n, int):
            if n < up_count:
                up_copy(n).start()
            elif n < up_count + down_count:
                down_copy(n - up_count).start()
            return

        @pl.when(n < up_count)
        def _():
            up_copy(n).start()

        @pl.when((n >= up_count) & (n < up_count + down_count))
        def _():
            down_copy(n - up_count).start()

    for n in range(slots):
        start_next(n)
    kept_copy(0).start()
    for side in range(hids):
        start = pl.multiple_of(side_start(side), width)
        for step in range(blocks):
            panel[step * each : (step + 1) * each, pl.ds(start, width)] = panel_refs[
                side * blocks + step
            ][...]
    chunk = even(shard, 1024)
    own = pl.ds(pl.multiple_of(me * width, width), skip * part)

    @pl.loop(0, shard // chunk)
    def _(c):
        columns = pl.ds(pl.multiple_of(c * chunk, chunk), chunk)
        up_sum[:, columns] = jnp.dot(
            panel[:, own], held_ref[:, columns], preferred_element_type=jnp.float32
        )

    def gate_act(columns):
        gate = jnp.dot(panel[...], gate_ref[:, columns], preferred_element_type=jnp.float32)
        return gate / (1.0 + jnp.exp(-gate))

    before = shard // chunk // 2

    @pl.loop(0, before)
    def _(c):
        columns = pl.ds(pl.multiple_of(c * chunk, chunk), chunk)
        act[:, columns] = gate_act(columns)

    @pl.loop(skip, hids * inside)
    def _(u):
        side, p = u // inside, u % inside
        x = panel[:, pl.ds(pl.multiple_of(side_start(side) + p * part, part), part)]
        for c in range(across):
            n = (u - skip) * across + c
            up_copy(n).wait()
            columns = slice(c * up_cols, (c + 1) * up_cols)
            up_sum[:, columns] += jnp.dot(
                x,
                ring[n % slots, 0:part, 0:up_cols],
                preferred_element_type=jnp.float32,
            )
            start_next(n + slots)

    kept_copy(1).start()

    @pl.loop(before, shard // chunk)
    def _(c):
        columns = pl.ds(pl.multiple_of(c * chunk, chunk), chunk)
        hidden_ref[:, columns] = (gate_act(columns) * up_sum[:, columns]).astype(jnp.bfloat16)

    done = slice(0, before * chunk)
    if before:
        hidden_ref[:, done] = (act[:, done] * up_sum[:, done]).astype(jnp.bfloat16)

    for side in range(1, hids):

        @pl.loop(0, wide)
        def _(c):
            total = None
            for k in range(deep):
                n = ((side - 1) * wide + c) * deep + k
                down_copy(n).wait()
                value = jnp.dot(
                    hidden_ref[:, k * down_rows : (k + 1) * down_rows],
                    ring[(n + up_count) % slots, 0:down_rows, 0:down_cols],
                    preferred_element_type=jnp.float32,
                )
                total = value if total is None else total + value
                start_next(n + up_count + slots)
            columns = pl.ds(pl.multiple_of(c * down_cols, 128), down_cols)
            out_refs[side - 1][:, columns] = total.astype(jnp.bfloat16)

    for n in range(2):
        kept_copy(n).wait()


def ffn(panels, gate_weight, up_held, up_weight, down_weight, blocks):
    hids = lax.axis_size("hid")
    each, width = panels[0].shape
    rows, depth = blocks * each, width * hids
    shard = gate_weight.shape[1]
    part, up_cols = even(width, 1024), even(shard, 1024)
    down_rows, down_cols = even(shard, 1024), even(width, 1024)
    slots = 6
    outs = [
        pltpu.VMEM((rows, shard), jnp.bfloat16),
        pltpu.VMEM((shard, (width // down_cols + 1) // 2 * down_cols), jnp.bfloat16),
    ] + [pltpu.VMEM((rows, width), jnp.bfloat16)] * (hids - 1)
    return pl.pallas_call(
        functools.partial(
            ffn_kernel, blocks, hids, (slots, part, up_cols, down_rows, down_cols)
        ),
        out_shape=tuple(outs),
        in_specs=[IN_VMEM] * (len(panels) + 2) + [ANYWHERE, ANYWHERE],
        out_specs=(IN_VMEM,) * (1 + hids),
        scratch_shapes=[
            pltpu.VMEM((rows, depth), jnp.bfloat16),
            pltpu.VMEM((rows, shard), jnp.float32),
            pltpu.VMEM((rows, max(128, shard // 2)), jnp.float32),
            pltpu.VMEM((slots, max(part, down_rows), max(up_cols, down_cols)), jnp.bfloat16),
            pltpu.SemaphoreType.DMA((slots,)),
            pltpu.SemaphoreType.DMA((2,)),
        ],
        compiler_params=pltpu.CompilerParams(vmem_limit_bytes=17 * MIB),
        cost_estimate=pl.CostEstimate(
            flops=4 * rows * depth * shard + 2 * rows * shard * (depth - width),
            bytes_accessed=4 * depth * shard,
            transcendentals=rows * shard,
        ),
        name="ffn",
    )(*panels, gate_weight, up_held, up_weight, down_weight)


def kept_kernel(hidden_ref, kept_ref, down_ref, out_ref, rest, sems):
    width = out_ref.shape[1]
    have, band = kept_ref.shape[1], rest.shape[2]
    me = lax.axis_index("hid")

    def copy(n):
        start = pl.multiple_of(me * width + have + n * band, 128)
        return pltpu.make_async_copy(
            down_ref.at[:, pl.ds(start, band)], rest.at[n], sems.at[n]
        )

    more = (width - have) // band
    for n in range(more):
        copy(n).start()

    @pl.loop(0, have // band)
    def _(n):
        columns = pl.ds(pl.multiple_of(n * band, 128), band)
        out_ref[:, columns] = jnp.dot(
            hidden_ref[...], kept_ref[:, columns], preferred_element_type=jnp.float32
        )

    @pl.loop(0, more)
    def _(n):
        copy(n).wait()
        columns = pl.ds(pl.multiple_of(have + n * band, 128), band)
        out_ref[:, columns] = jnp.dot(
            hidden_ref[...], rest[n], preferred_element_type=jnp.float32
        )


def kept_part(hidden, kept, down_weight):
    rows, shard = hidden.shape
    width = down_weight.shape[1] // lax.axis_size("hid")
    band = even(kept.shape[1], 512)
    more = max(1, (width - kept.shape[1]) // band)
    return pl.pallas_call(
        kept_kernel,
        out_shape=jax.ShapeDtypeStruct((rows, width), jnp.float32),
        in_specs=[IN_VMEM, IN_VMEM, ANYWHERE],
        out_specs=IN_VMEM,
        scratch_shapes=[
            pltpu.VMEM((more, shard, band), jnp.bfloat16),
            pltpu.SemaphoreType.DMA((more,)),
        ],
        compiler_params=pltpu.CompilerParams(vmem_limit_bytes=6 * MIB),
        cost_estimate=pl.CostEstimate(
            flops=2 * rows * shard * width, bytes_accessed=2 * shard * width, transcendentals=0
        ),
        name="kept_part",
    )(hidden, kept, down_weight)


def hid_sum_kernel(count, *refs):
    total = refs[0][...]
    for ref in refs[1:count]:
        total += ref[...].astype(jnp.float32)
    each = total.shape[0] // len(refs[count:])
    for step, ref in enumerate(refs[count:]):
        ref[...] = total[step * each : (step + 1) * each, :].astype(ref.dtype)


def hid_sum(parts, blocks):
    rows, width = parts[0].shape
    each = rows // blocks
    outs = [jax.ShapeDtypeStruct((each, width), jnp.float32)]
    outs += [jax.ShapeDtypeStruct((each, width), jnp.bfloat16)] * (blocks - 1)
    return pl.pallas_call(
        functools.partial(hid_sum_kernel, len(parts)),
        out_shape=tuple(outs),
        in_specs=[IN_VMEM] * len(parts),
        out_specs=(IN_VMEM,) * blocks,
        compiler_params=pltpu.CompilerParams(vmem_limit_bytes=4 * MIB),
        name="hid_sum",
    )(*parts)


def blk_sum_kernel(*refs):
    total = refs[0][...]
    for ref in refs[1:-1]:
        total += ref[...].astype(jnp.float32)
    refs[-1][...] = total.astype(refs[-1].dtype)


def blk_sum(parts):
    return pl.pallas_call(
        blk_sum_kernel,
        out_shape=jax.ShapeDtypeStruct(parts[0].shape, jnp.bfloat16),
        in_specs=[IN_VMEM] * len(parts),
        out_specs=IN_VMEM,
        compiler_params=pltpu.CompilerParams(vmem_limit_bytes=4 * MIB),
        name="blk_sum",
    )(*parts)


def held(array):
    return pltpu.with_memory_space_constraint(array, pltpu.VMEM)


def on_device(tokens, kinds, slots, gains, gate_weight, up_weight, down_weight):
    blocks, lanes, hids = (lax.axis_size(axis) for axis in ("blk", "regroup", "hid"))
    tokens, kinds, slots, gains, up_weight, down_weight = (
        pltpu.with_memory_space_constraint(array, pltpu.HBM)
        for array in (tokens, kinds, slots, gains, up_weight, down_weight)
    )
    gate_weight = held(gate_weight)
    pieces = norm(tokens, kinds, slots, gains)
    half = arrange(
        [pieces[0]] + [exchange(pieces[step], "regroup", step) for step in range(1, lanes)]
    )
    halves = [half] + [exchange(half, "blk", step) for step in range(1, blocks)]
    up_held = early(half, up_weight)
    for step in range(1, blocks):
        halves[step], up_held = lax.optimization_barrier((halves[step], up_held))
    panels = halves + [exchange(part, "hid", side) for side in range(1, hids) for part in halves]
    panels = [held(part) for part in panels]
    up_held = held(up_held)
    hidden, kept, *sent = ffn(panels, gate_weight, up_held, up_weight, down_weight, blocks)
    hidden, kept = held(hidden), held(kept)
    came = [exchange(part, "hid", step + 1) for step, part in enumerate(sent)]
    parts = hid_sum([kept_part(hidden, kept, down_weight)] + came, blocks)
    return blk_sum(
        [parts[0]] + [exchange(parts[step], "blk", step) for step in range(1, blocks)]
    )


def solution(mesh):
    placed = (
        P(("blk", "regroup"), None),
        P(("blk", "regroup")),
        P(("blk", "regroup"), None),
        P(),
        P(None, ("blk", "hid")),
        P(None, ("blk", "hid")),
        P(("blk", "hid"), None),
    )
    return jax.shard_map(
        on_device,
        mesh=mesh,
        in_specs=placed,
        out_specs=P(("blk", "regroup"), "hid"),
        check_vma=False,
    )
```

```python
import functools

import jax
import jax.numpy as jnp
from jax import lax
from jax.experimental import pallas as pl
from jax.experimental.pallas import tpu as pltpu
from jax.sharding import PartitionSpec as P

epsilon = 1e-05
MIB = 1 << 20

ANYWHERE = pl.BlockSpec(memory_space=pl.ANY)
IN_VMEM = pl.BlockSpec(memory_space=pltpu.VMEM)


def log2(number):
    bits = number.bit_length() - 1
    assert 1 << bits == number
    return bits


def exchange(array, axis, step):
    count = lax.axis_size(axis)
    log2(count)
    return lax.ppermute(array, axis, [(i, i ^ step) for i in range(count)])


def norm_kernel(lanes, hids, *refs):
    count = lanes // hids
    sources, piece_refs = refs[:4], refs[4 : 4 + count]
    targets, placed, sems = refs[4 + count : 8 + count], refs[8 + count], refs[9 + count]
    copies = [
        pltpu.make_async_copy(src, dst, sems.at[i])
        for i, (src, dst) in enumerate(zip(sources, targets))
    ]
    for copy in copies:
        copy.start()
    for copy in copies:
        copy.wait()
    tokens_ref, kinds_ref, slots_ref, gains_ref = targets
    rows = tokens_ref.shape[0]
    rounds = rows // lanes
    x = tokens_ref[...].astype(jnp.float32)
    row_scale = lax.rsqrt(jnp.mean(x * x, axis=1, keepdims=True) + epsilon)
    at = lax.broadcasted_iota(jnp.int32, (rows, 1), 0)
    kind = jnp.zeros((rows, 1), jnp.int32)
    for i in range(rows):
        kind = jnp.where(at == i, kinds_ref[i], kind)
    gain = jnp.broadcast_to(gains_ref[0:1, :], x.shape)
    for c in range(1, gains_ref.shape[0]):
        gain = jnp.where(kind == c, gains_ref[c : c + 1, :], gain)
    normed = (x * row_scale * gain).astype(jnp.bfloat16)
    target = lax.broadcasted_iota(jnp.int32, (count * rounds, rows), 0)
    step = lax.axis_index("hid") * count + lax.shift_right_logical(target, log2(rounds))
    lane = jnp.bitwise_xor(step, lax.axis_index("regroup"))
    slot = jnp.bitwise_and(target, rounds - 1) * lanes + lane
    placing = (jnp.broadcast_to(slots_ref[0:1, :], slot.shape) == slot).astype(jnp.bfloat16)
    placed[...] = jnp.dot(placing, normed, preferred_element_type=jnp.float32)
    for t, ref in enumerate(piece_refs):
        ref[...] = placed[t * rounds : (t + 1) * rounds, :].astype(jnp.bfloat16)


def norm(tokens, kinds, slots, gains):
    rows, features = tokens.shape
    lanes, hids = lax.axis_size("regroup"), lax.axis_size("hid")
    count, rounds = lanes // hids, rows // lanes
    return pl.pallas_call(
        functools.partial(norm_kernel, lanes, hids),
        out_shape=(jax.ShapeDtypeStruct((rounds, features), jnp.bfloat16),) * count,
        in_specs=[ANYWHERE] * 4,
        out_specs=(IN_VMEM,) * count,
        scratch_shapes=[
            pltpu.VMEM(tokens.shape, tokens.dtype),
            pltpu.SMEM(kinds.shape, kinds.dtype),
            pltpu.VMEM(slots.shape, slots.dtype),
            pltpu.VMEM(gains.shape, gains.dtype),
            pltpu.VMEM((count * rounds, features), jnp.float32),
            pltpu.SemaphoreType.DMA((4,)),
        ],
        compiler_params=pltpu.CompilerParams(vmem_limit_bytes=4 * MIB),
        cost_estimate=pl.CostEstimate(flops=0, bytes_accessed=48 * MIB, transcendentals=0),
        name="norm",
    )(tokens, kinds, slots, gains)


def to_lanes(pieces):
    lanes, hids = lax.axis_size("regroup"), lax.axis_size("hid")
    count = len(pieces)
    assert count * hids == lanes

    def pairs(t):
        for lane in range(lanes):
            for core in range(hids):
                yield lane * hids + core, (lane ^ (core * count + t)) * hids + core

    return [lax.ppermute(piece, ("regroup", "hid"), list(pairs(t))) for t, piece in enumerate(pieces)]


def stack_kernel(*refs):
    *piece_refs, out_ref, stack = refs
    rounds = piece_refs[0].shape[0]
    for t, ref in enumerate(piece_refs):
        stack[t * rounds : (t + 1) * rounds, :] = ref[...].astype(jnp.float32)
    out_ref[...] = stack[...].astype(jnp.bfloat16)


def stacked(pieces):
    rounds, width = pieces[0].shape
    rows = len(pieces) * rounds
    return pl.pallas_call(
        stack_kernel,
        out_shape=jax.ShapeDtypeStruct((rows, width), jnp.bfloat16),
        in_specs=[IN_VMEM] * len(pieces),
        out_specs=IN_VMEM,
        scratch_shapes=[pltpu.VMEM((rows, width), jnp.float32)],
        compiler_params=pltpu.CompilerParams(vmem_limit_bytes=4 * MIB),
        name="stacked",
    )(*pieces)


def even(total, most):
    return next(size for size in range(min(most, total), 0, -128) if total % size == 0)


def early_kernel(width, after_ref, up_ref, out_ref, sem):
    start = pl.multiple_of(lax.axis_index("hid") * width, width)
    copy = pltpu.make_async_copy(up_ref.at[pl.ds(start, out_ref.shape[0]), :], out_ref, sem)
    copy.start()
    copy.wait()


def early(after, up_weight):
    width = up_weight.shape[0] // lax.axis_size("hid")
    depth = width - even(width, 1024)
    shard = up_weight.shape[1]
    return pl.pallas_call(
        functools.partial(early_kernel, width),
        out_shape=pltpu.VMEM((depth, shard), jnp.bfloat16),
        in_specs=[ANYWHERE, ANYWHERE],
        out_specs=IN_VMEM,
        scratch_shapes=[pltpu.SemaphoreType.DMA(())],
        compiler_params=pltpu.CompilerParams(vmem_limit_bytes=1 * MIB),
        cost_estimate=pl.CostEstimate(
            flops=0, bytes_accessed=2 * depth * shard, transcendentals=0
        ),
        name="early",
    )(after, up_weight)


def ffn_kernel(blocks, hids, plan, *refs):
    slots, part, up_cols, down_rows, down_cols = plan
    count = blocks * hids
    panel_refs = refs[:count]
    gate_ref, held_ref, up_ref, down_ref = refs[count : count + 4]
    hidden_ref, kept = refs[count + 4 : count + 6]
    out_refs = refs[count + 6 : count + 5 + hids]
    panel, up_sum, act, ring, ring_sems, kept_sems = refs[count + 5 + hids :]
    rows, depth = panel.shape
    each = rows // blocks
    shard = gate_ref.shape[1]
    width = depth // hids
    me = lax.axis_index("hid")
    inside, across = width // part, shard // up_cols
    deep, wide = shard // down_rows, width // down_cols
    skip = held_ref.shape[0] // part
    up_count = (hids * inside - skip) * across
    down_count = (hids - 1) * wide * deep

    def side_start(side):
        return jnp.bitwise_xor(me, side) * width

    def up_copy(n):
        u, c = n // across + skip, n % across
        side, p = u // inside, u % inside
        return pltpu.make_async_copy(
            up_ref.at[
                pl.ds(pl.multiple_of(side_start(side) + p * part, part), part),
                pl.ds(pl.multiple_of(c * up_cols, up_cols), up_cols),
            ],
            ring.at[n % slots, pl.ds(0, part), pl.ds(0, up_cols)],
            ring_sems.at[n % slots],
        )

    def down_copy(n):
        side, c, k = n // (wide * deep) + 1, n // deep % wide, n % deep
        slot = (n + up_count) % slots
        return pltpu.make_async_copy(
            down_ref.at[
                pl.ds(pl.multiple_of(k * down_rows, down_rows), down_rows),
                pl.ds(pl.multiple_of(side_start(side) + c * down_cols, 128), down_cols),
            ],
            ring.at[slot, pl.ds(0, down_rows), pl.ds(0, down_cols)],
            ring_sems.at[slot],
        )

    def kept_copy(n):
        size = kept.shape[1] // 2
        start = pl.multiple_of(me * width + n * size, 128)
        return pltpu.make_async_copy(
            down_ref.at[:, pl.ds(start, size)],
            kept.at[:, n * size : (n + 1) * size],
            kept_sems.at[n],
        )

    def start_next(n):
        if isinstance(n, int):
            if n < up_count:
                up_copy(n).start()
            elif n < up_count + down_count:
                down_copy(n - up_count).start()
            return

        @pl.when(n < up_count)
        def _():
            up_copy(n).start()

        @pl.when((n >= up_count) & (n < up_count + down_count))
        def _():
            down_copy(n - up_count).start()

    for n in range(slots):
        start_next(n)
    kept_copy(0).start()
    cores = lax.broadcasted_iota(jnp.int32, (each // hids, 1), 0) * 0 + me
    for step in range(blocks):
        sides = [
            panel_refs[side * blocks + step][...].astype(jnp.float32) for side in range(hids)
        ]
        lined = []
        for core in range(hids):
            rows_of = sides[core]
            for mine in range(1, hids):
                rows_of = jnp.where(cores == mine, sides[core ^ mine], rows_of)
            lined.append(rows_of)
        panel[step * each : (step + 1) * each, :] = jnp.concatenate(lined, axis=0).astype(
            jnp.bfloat16
        )
    chunk = even(shard, 1024)
    own = pl.ds(pl.multiple_of(me * width, width), skip * part)

    @pl.loop(0, shard // chunk)
    def _(c):
        columns = pl.ds(pl.multiple_of(c * chunk, chunk), chunk)
        up_sum[:, columns] = jnp.dot(
            panel[:, own], held_ref[:, columns], preferred_element_type=jnp.float32
        )

    def gate_act(columns):
        gate = jnp.dot(panel[...], gate_ref[:, columns], preferred_element_type=jnp.float32)
        return gate / (1.0 + jnp.exp(-gate))

    before = shard // chunk // 2

    @pl.loop(0, before)
    def _(c):
        columns = pl.ds(pl.multiple_of(c * chunk, chunk), chunk)
        act[:, columns] = gate_act(columns)

    @pl.loop(skip, hids * inside)
    def _(u):
        side, p = u // inside, u % inside
        x = panel[:, pl.ds(pl.multiple_of(side_start(side) + p * part, part), part)]
        for c in range(across):
            n = (u - skip) * across + c
            up_copy(n).wait()
            columns = slice(c * up_cols, (c + 1) * up_cols)
            up_sum[:, columns] += jnp.dot(
                x,
                ring[n % slots, 0:part, 0:up_cols],
                preferred_element_type=jnp.float32,
            )
            start_next(n + slots)

    kept_copy(1).start()

    @pl.loop(before, shard // chunk)
    def _(c):
        columns = pl.ds(pl.multiple_of(c * chunk, chunk), chunk)
        hidden_ref[:, columns] = (gate_act(columns) * up_sum[:, columns]).astype(jnp.bfloat16)

    done = slice(0, before * chunk)
    if before:
        hidden_ref[:, done] = (act[:, done] * up_sum[:, done]).astype(jnp.bfloat16)

    for side in range(1, hids):

        @pl.loop(0, wide)
        def _(c):
            total = None
            for k in range(deep):
                down_copy(((side - 1) * wide + c) * deep + k).wait()
            for k in range(deep):
                n = ((side - 1) * wide + c) * deep + k
                value = jnp.dot(
                    hidden_ref[:, k * down_rows : (k + 1) * down_rows],
                    ring[(n + up_count) % slots, 0:down_rows, 0:down_cols],
                    preferred_element_type=jnp.float32,
                )
                total = value if total is None else total + value
            for k in range(deep):
                start_next(((side - 1) * wide + c) * deep + k + up_count + slots)
            columns = pl.ds(pl.multiple_of(c * down_cols, 128), down_cols)
            out_refs[side - 1][:, columns] = total.astype(jnp.bfloat16)

    for n in range(2):
        kept_copy(n).wait()


def ffn(panels, gate_weight, up_held, up_weight, down_weight, blocks):
    hids = lax.axis_size("hid")
    each, depth = panels[0].shape
    rows, width = blocks * hids * each, depth // hids
    shard = gate_weight.shape[1]
    part, up_cols = even(width, 1024), even(shard, 1024)
    down_rows, down_cols = even(shard, 1024), even(width, 1024)
    slots = 6
    outs = [
        pltpu.VMEM((rows, shard), jnp.bfloat16),
        pltpu.VMEM((shard, (width // down_cols + 1) // 2 * down_cols), jnp.bfloat16),
    ] + [pltpu.VMEM((rows, width), jnp.bfloat16)] * (hids - 1)
    return pl.pallas_call(
        functools.partial(
            ffn_kernel, blocks, hids, (slots, part, up_cols, down_rows, down_cols)
        ),
        out_shape=tuple(outs),
        in_specs=[IN_VMEM] * (len(panels) + 2) + [ANYWHERE, ANYWHERE],
        out_specs=(IN_VMEM,) * (1 + hids),
        scratch_shapes=[
            pltpu.VMEM((rows, depth), jnp.bfloat16),
            pltpu.VMEM((rows, shard), jnp.float32),
            pltpu.VMEM((rows, max(128, shard // 2)), jnp.float32),
            pltpu.VMEM((slots, max(part, down_rows), max(up_cols, down_cols)), jnp.bfloat16),
            pltpu.SemaphoreType.DMA((slots,)),
            pltpu.SemaphoreType.DMA((2,)),
        ],
        compiler_params=pltpu.CompilerParams(vmem_limit_bytes=17 * MIB),
        cost_estimate=pl.CostEstimate(
            flops=4 * rows * depth * shard + 2 * rows * shard * (depth - width),
            bytes_accessed=4 * depth * shard,
            transcendentals=rows * shard,
        ),
        name="ffn",
    )(*panels, gate_weight, up_held, up_weight, down_weight)


def kept_kernel(hidden_ref, kept_ref, down_ref, out_ref, rest, sems):
    width = out_ref.shape[1]
    have, band = kept_ref.shape[1], rest.shape[2]
    me = lax.axis_index("hid")

    def copy(n):
        start = pl.multiple_of(me * width + have + n * band, 128)
        return pltpu.make_async_copy(
            down_ref.at[:, pl.ds(start, band)], rest.at[n], sems.at[n]
        )

    more = (width - have) // band
    for n in range(more):
        copy(n).start()

    @pl.loop(0, have // band)
    def _(n):
        columns = pl.ds(pl.multiple_of(n * band, 128), band)
        out_ref[:, columns] = jnp.dot(
            hidden_ref[...], kept_ref[:, columns], preferred_element_type=jnp.float32
        )

    @pl.loop(0, more)
    def _(n):
        copy(n).wait()
        columns = pl.ds(pl.multiple_of(have + n * band, 128), band)
        out_ref[:, columns] = jnp.dot(
            hidden_ref[...], rest[n], preferred_element_type=jnp.float32
        )


def kept_part(hidden, kept, down_weight):
    rows, shard = hidden.shape
    width = down_weight.shape[1] // lax.axis_size("hid")
    band = even(kept.shape[1], 512)
    more = max(1, (width - kept.shape[1]) // band)
    return pl.pallas_call(
        kept_kernel,
        out_shape=jax.ShapeDtypeStruct((rows, width), jnp.float32),
        in_specs=[IN_VMEM, IN_VMEM, ANYWHERE],
        out_specs=IN_VMEM,
        scratch_shapes=[
            pltpu.VMEM((more, shard, band), jnp.bfloat16),
            pltpu.SemaphoreType.DMA((more,)),
        ],
        compiler_params=pltpu.CompilerParams(vmem_limit_bytes=6 * MIB),
        cost_estimate=pl.CostEstimate(
            flops=2 * rows * shard * width, bytes_accessed=2 * shard * width, transcendentals=0
        ),
        name="kept_part",
    )(hidden, kept, down_weight)


def hid_sum_kernel(count, *refs):
    total = refs[0][...]
    for ref in refs[1:count]:
        total += ref[...].astype(jnp.float32)
    each = total.shape[0] // len(refs[count:])
    for step, ref in enumerate(refs[count:]):
        ref[...] = total[step * each : (step + 1) * each, :].astype(ref.dtype)


def hid_sum(parts, blocks):
    rows, width = parts[0].shape
    each = rows // blocks
    outs = [jax.ShapeDtypeStruct((each, width), jnp.float32)]
    outs += [jax.ShapeDtypeStruct((each, width), jnp.bfloat16)] * (blocks - 1)
    return pl.pallas_call(
        functools.partial(hid_sum_kernel, len(parts)),
        out_shape=tuple(outs),
        in_specs=[IN_VMEM] * len(parts),
        out_specs=(IN_VMEM,) * blocks,
        compiler_params=pltpu.CompilerParams(vmem_limit_bytes=4 * MIB),
        name="hid_sum",
    )(*parts)


def blk_sum_kernel(lanes, *refs):
    *part_refs, out_ref = refs
    total = part_refs[0][...]
    for ref in part_refs[1:]:
        total += ref[...].astype(jnp.float32)
    rows = out_ref.shape[0]
    rounds = rows // lanes
    r = lax.broadcasted_iota(jnp.int32, (rows, rows), 0)
    c = lax.broadcasted_iota(jnp.int32, (rows, rows), 1)
    step = jnp.bitwise_xor(jnp.bitwise_and(r, lanes - 1), lax.axis_index("regroup"))
    order = (c == step * rounds + lax.shift_right_logical(r, log2(lanes))).astype(jnp.bfloat16)
    out_ref[...] = jnp.dot(
        order, total.astype(jnp.bfloat16), preferred_element_type=jnp.float32
    ).astype(jnp.bfloat16)


def blk_sum(parts):
    return pl.pallas_call(
        functools.partial(blk_sum_kernel, lax.axis_size("regroup")),
        out_shape=jax.ShapeDtypeStruct(parts[0].shape, jnp.bfloat16),
        in_specs=[IN_VMEM] * len(parts),
        out_specs=IN_VMEM,
        compiler_params=pltpu.CompilerParams(vmem_limit_bytes=4 * MIB),
        name="blk_sum",
    )(*parts)


def held(array):
    return pltpu.with_memory_space_constraint(array, pltpu.VMEM)


def on_device(tokens, kinds, slots, gains, gate_weight, up_weight, down_weight):
    blocks, lanes, hids = (lax.axis_size(axis) for axis in ("blk", "regroup", "hid"))
    tokens, kinds, slots, gains, up_weight, down_weight = (
        pltpu.with_memory_space_constraint(array, pltpu.HBM)
        for array in (tokens, kinds, slots, gains, up_weight, down_weight)
    )
    gate_weight = held(gate_weight)
    half = stacked(to_lanes(norm(tokens, kinds, slots, gains)))
    halves = [half] + [exchange(half, "blk", step) for step in range(1, blocks)]
    up_held = early(half, up_weight)
    for step in range(1, blocks):
        halves[step], up_held = lax.optimization_barrier((halves[step], up_held))
    panels = halves + [exchange(part, "hid", side) for side in range(1, hids) for part in halves]
    panels = [held(part) for part in panels]
    up_held = held(up_held)
    hidden, kept, *sent = ffn(panels, gate_weight, up_held, up_weight, down_weight, blocks)
    hidden, kept = held(hidden), held(kept)
    came = [exchange(part, "hid", step + 1) for step, part in enumerate(sent)]
    parts = hid_sum([kept_part(hidden, kept, down_weight)] + came, blocks)
    return blk_sum(
        [parts[0]] + [exchange(parts[step], "blk", step) for step in range(1, blocks)]
    )


def solution(mesh):
    placed = (
        P(("blk", "regroup"), None),
        P(("blk", "regroup")),
        P(("blk", "regroup"), None),
        P(),
        P(None, ("blk", "hid")),
        P(None, ("blk", "hid")),
        P(("blk", "hid"), None),
    )
    return jax.shard_map(
        on_device,
        mesh=mesh,
        in_specs=placed,
        out_specs=P(("blk", "regroup"), "hid"),
        check_vma=False,
    )
```

```python
import functools

import jax
import jax.numpy as jnp
from jax import lax
from jax.experimental import pallas as pl
from jax.experimental.pallas import tpu as pltpu
from jax.sharding import PartitionSpec as P

epsilon = 1e-05
MIB = 1 << 20

ANYWHERE = pl.BlockSpec(memory_space=pl.ANY)
IN_VMEM = pl.BlockSpec(memory_space=pltpu.VMEM)


def log2(number):
    bits = number.bit_length() - 1
    assert 1 << bits == number
    return bits


def exchange(array, axis, step):
    count = lax.axis_size(axis)
    log2(count)
    return lax.ppermute(array, axis, [(i, i ^ step) for i in range(count)])


def norm_kernel(lanes, hids, *refs):
    count = lanes // hids
    sources, piece_refs = refs[:4], refs[4 : 4 + count]
    targets, placed, sems = refs[4 + count : 8 + count], refs[8 + count], refs[9 + count]
    copies = [
        pltpu.make_async_copy(src, dst, sems.at[i])
        for i, (src, dst) in enumerate(zip(sources, targets))
    ]
    for copy in copies:
        copy.start()
    for copy in copies:
        copy.wait()
    tokens_ref, kinds_ref, slots_ref, gains_ref = targets
    rows = tokens_ref.shape[0]
    rounds = rows // lanes
    x = tokens_ref[...].astype(jnp.float32)
    row_scale = lax.rsqrt(jnp.mean(x * x, axis=1, keepdims=True) + epsilon)
    at = lax.broadcasted_iota(jnp.int32, (rows, 1), 0)
    kind = jnp.zeros((rows, 1), jnp.int32)
    for i in range(rows):
        kind = jnp.where(at == i, kinds_ref[i], kind)
    gain = jnp.broadcast_to(gains_ref[0:1, :], x.shape)
    for c in range(1, gains_ref.shape[0]):
        gain = jnp.where(kind == c, gains_ref[c : c + 1, :], gain)
    normed = (x * row_scale * gain).astype(jnp.bfloat16)
    target = lax.broadcasted_iota(jnp.int32, (count * rounds, rows), 0)
    turn = lax.shift_right_logical(target, log2(rounds))
    step = turn * hids + lax.axis_index("hid")
    lane = jnp.bitwise_xor(step, lax.axis_index("regroup"))
    slot = jnp.bitwise_and(target, rounds - 1) * lanes + lane
    placing = (jnp.broadcast_to(slots_ref[0:1, :], slot.shape) == slot).astype(jnp.bfloat16)
    placed[...] = jnp.dot(placing, normed, preferred_element_type=jnp.float32)
    for t, ref in enumerate(piece_refs):
        ref[...] = placed[t * rounds : (t + 1) * rounds, :].astype(jnp.bfloat16)


def norm(tokens, kinds, slots, gains):
    rows, features = tokens.shape
    lanes, hids = lax.axis_size("regroup"), lax.axis_size("hid")
    count, rounds = lanes // hids, rows // lanes
    return pl.pallas_call(
        functools.partial(norm_kernel, lanes, hids),
        out_shape=(jax.ShapeDtypeStruct((rounds, features), jnp.bfloat16),) * count,
        in_specs=[ANYWHERE] * 4,
        out_specs=(IN_VMEM,) * count,
        scratch_shapes=[
            pltpu.VMEM(tokens.shape, tokens.dtype),
            pltpu.SMEM(kinds.shape, kinds.dtype),
            pltpu.VMEM(slots.shape, slots.dtype),
            pltpu.VMEM(gains.shape, gains.dtype),
            pltpu.VMEM((count * rounds, features), jnp.float32),
            pltpu.SemaphoreType.DMA((4,)),
        ],
        compiler_params=pltpu.CompilerParams(vmem_limit_bytes=4 * MIB),
        cost_estimate=pl.CostEstimate(flops=0, bytes_accessed=48 * MIB, transcendentals=0),
        name="norm",
    )(tokens, kinds, slots, gains)


def to_lanes(pieces):
    lanes, hids = lax.axis_size("regroup"), lax.axis_size("hid")
    count = len(pieces)
    assert count * hids == lanes

    def pairs(t):
        for lane in range(lanes):
            for core in range(hids):
                yield lane * hids + core, (lane ^ (t * hids + core)) * hids + core

    return [lax.ppermute(piece, ("regroup", "hid"), list(pairs(t))) for t, piece in enumerate(pieces)]


def stack_kernel(*refs):
    *piece_refs, out_ref, stack = refs
    rounds = piece_refs[0].shape[0]
    for t, ref in enumerate(piece_refs):
        stack[t * rounds : (t + 1) * rounds, :] = ref[...].astype(jnp.float32)
    out_ref[...] = stack[...].astype(jnp.bfloat16)


def stacked(pieces):
    rounds, width = pieces[0].shape
    rows = len(pieces) * rounds
    return pl.pallas_call(
        stack_kernel,
        out_shape=jax.ShapeDtypeStruct((rows, width), jnp.bfloat16),
        in_specs=[IN_VMEM] * len(pieces),
        out_specs=IN_VMEM,
        scratch_shapes=[pltpu.VMEM((rows, width), jnp.float32)],
        compiler_params=pltpu.CompilerParams(vmem_limit_bytes=4 * MIB),
        name="stacked",
    )(*pieces)


def even(total, most):
    return next(size for size in range(min(most, total), 0, -128) if total % size == 0)


def early_kernel(width, after_ref, up_ref, out_ref, sem):
    start = pl.multiple_of(lax.axis_index("hid") * width, width)
    copy = pltpu.make_async_copy(up_ref.at[pl.ds(start, out_ref.shape[0]), :], out_ref, sem)
    copy.start()
    copy.wait()


def early(after, up_weight):
    width = up_weight.shape[0] // lax.axis_size("hid")
    depth = width - even(width, 1024)
    shard = up_weight.shape[1]
    return pl.pallas_call(
        functools.partial(early_kernel, width),
        out_shape=pltpu.VMEM((depth, shard), jnp.bfloat16),
        in_specs=[ANYWHERE, ANYWHERE],
        out_specs=IN_VMEM,
        scratch_shapes=[pltpu.SemaphoreType.DMA(())],
        compiler_params=pltpu.CompilerParams(vmem_limit_bytes=1 * MIB),
        cost_estimate=pl.CostEstimate(
            flops=0, bytes_accessed=2 * depth * shard, transcendentals=0
        ),
        name="early",
    )(after, up_weight)


def ffn_kernel(blocks, hids, plan, *refs):
    slots, part, up_cols, down_rows, down_cols = plan
    count = blocks * hids
    panel_refs = refs[:count]
    gate_ref, held_ref, up_ref, down_ref = refs[count : count + 4]
    hidden_ref, kept = refs[count + 4 : count + 6]
    out_refs = refs[count + 6 : count + 5 + hids]
    panel, up_sum, act, ring, ring_sems, kept_sems = refs[count + 5 + hids :]
    rows, depth = panel.shape
    each = rows // blocks
    shard = gate_ref.shape[1]
    width = depth // hids
    me = lax.axis_index("hid")
    inside, across = width // part, shard // up_cols
    deep, wide = shard // down_rows, width // down_cols
    skip = held_ref.shape[0] // part
    up_count = (hids * inside - skip) * across
    down_count = (hids - 1) * wide * deep

    def side_start(side):
        return jnp.bitwise_xor(me, side) * width

    def up_copy(n):
        u, c = n // across + skip, n % across
        side, p = u // inside, u % inside
        return pltpu.make_async_copy(
            up_ref.at[
                pl.ds(pl.multiple_of(side_start(side) + p * part, part), part),
                pl.ds(pl.multiple_of(c * up_cols, up_cols), up_cols),
            ],
            ring.at[n % slots, pl.ds(0, part), pl.ds(0, up_cols)],
            ring_sems.at[n % slots],
        )

    def down_copy(n):
        side, c, k = n // (wide * deep) + 1, n // deep % wide, n % deep
        slot = (n + up_count) % slots
        return pltpu.make_async_copy(
            down_ref.at[
                pl.ds(pl.multiple_of(k * down_rows, down_rows), down_rows),
                pl.ds(pl.multiple_of(side_start(side) + c * down_cols, 128), down_cols),
            ],
            ring.at[slot, pl.ds(0, down_rows), pl.ds(0, down_cols)],
            ring_sems.at[slot],
        )

    def kept_copy(n):
        size = kept.shape[1] // 2
        start = pl.multiple_of(me * width + n * size, 128)
        return pltpu.make_async_copy(
            down_ref.at[:, pl.ds(start, size)],
            kept.at[:, n * size : (n + 1) * size],
            kept_sems.at[n],
        )

    def start_next(n):
        if isinstance(n, int):
            if n < up_count:
                up_copy(n).start()
            elif n < up_count + down_count:
                down_copy(n - up_count).start()
            return

        @pl.when(n < up_count)
        def _():
            up_copy(n).start()

        @pl.when((n >= up_count) & (n < up_count + down_count))
        def _():
            down_copy(n - up_count).start()

    for n in range(slots):
        start_next(n)
    kept_copy(0).start()
    cores = lax.broadcasted_iota(jnp.int32, (each // hids, 1), 0) * 0 + me
    for step in range(blocks):
        sides = [
            panel_refs[side * blocks + step][...].astype(jnp.float32) for side in range(hids)
        ]
        lined = []
        for core in range(hids):
            rows_of = sides[core]
            for mine in range(1, hids):
                rows_of = jnp.where(cores == mine, sides[core ^ mine], rows_of)
            lined.append(rows_of)
        panel[step * each : (step + 1) * each, :] = jnp.concatenate(lined, axis=0).astype(
            jnp.bfloat16
        )
    chunk = even(shard, 1024)
    own = pl.ds(pl.multiple_of(me * width, width), skip * part)

    @pl.loop(0, shard // chunk)
    def _(c):
        columns = pl.ds(pl.multiple_of(c * chunk, chunk), chunk)
        up_sum[:, columns] = jnp.dot(
            panel[:, own], held_ref[:, columns], preferred_element_type=jnp.float32
        )

    def gate_act(columns):
        gate = jnp.dot(panel[...], gate_ref[:, columns], preferred_element_type=jnp.float32)
        return gate / (1.0 + jnp.exp(-gate))

    before = shard // chunk // 2

    @pl.loop(0, before)
    def _(c):
        columns = pl.ds(pl.multiple_of(c * chunk, chunk), chunk)
        act[:, columns] = gate_act(columns)

    @pl.loop(skip, hids * inside)
    def _(u):
        side, p = u // inside, u % inside
        x = panel[:, pl.ds(pl.multiple_of(side_start(side) + p * part, part), part)]
        for c in range(across):
            n = (u - skip) * across + c
            up_copy(n).wait()
            columns = slice(c * up_cols, (c + 1) * up_cols)
            up_sum[:, columns] += jnp.dot(
                x,
                ring[n % slots, 0:part, 0:up_cols],
                preferred_element_type=jnp.float32,
            )
            start_next(n + slots)

    kept_copy(1).start()

    @pl.loop(before, shard // chunk)
    def _(c):
        columns = pl.ds(pl.multiple_of(c * chunk, chunk), chunk)
        hidden_ref[:, columns] = (gate_act(columns) * up_sum[:, columns]).astype(jnp.bfloat16)

    done = slice(0, before * chunk)
    if before:
        hidden_ref[:, done] = (act[:, done] * up_sum[:, done]).astype(jnp.bfloat16)

    for side in range(1, hids):

        @pl.loop(0, wide)
        def _(c):
            total = None
            for k in range(deep):
                down_copy(((side - 1) * wide + c) * deep + k).wait()
            for k in range(deep):
                n = ((side - 1) * wide + c) * deep + k
                value = jnp.dot(
                    hidden_ref[:, k * down_rows : (k + 1) * down_rows],
                    ring[(n + up_count) % slots, 0:down_rows, 0:down_cols],
                    preferred_element_type=jnp.float32,
                )
                total = value if total is None else total + value
            for k in range(deep):
                start_next(((side - 1) * wide + c) * deep + k + up_count + slots)
            columns = pl.ds(pl.multiple_of(c * down_cols, 128), down_cols)
            out_refs[side - 1][:, columns] = total.astype(jnp.bfloat16)

    for n in range(2):
        kept_copy(n).wait()


def ffn(panels, gate_weight, up_held, up_weight, down_weight, blocks):
    hids = lax.axis_size("hid")
    each, depth = panels[0].shape
    rows, width = blocks * hids * each, depth // hids
    shard = gate_weight.shape[1]
    part, up_cols = even(width, 1024), even(shard, 1024)
    down_rows, down_cols = even(shard, 1024), even(width, 1024)
    slots = 6
    outs = [
        pltpu.VMEM((rows, shard), jnp.bfloat16),
        pltpu.VMEM((shard, (width // down_cols + 1) // 2 * down_cols), jnp.bfloat16),
    ] + [pltpu.VMEM((rows, width), jnp.bfloat16)] * (hids - 1)
    return pl.pallas_call(
        functools.partial(
            ffn_kernel, blocks, hids, (slots, part, up_cols, down_rows, down_cols)
        ),
        out_shape=tuple(outs),
        in_specs=[IN_VMEM] * (len(panels) + 2) + [ANYWHERE, ANYWHERE],
        out_specs=(IN_VMEM,) * (1 + hids),
        scratch_shapes=[
            pltpu.VMEM((rows, depth), jnp.bfloat16),
            pltpu.VMEM((rows, shard), jnp.float32),
            pltpu.VMEM((rows, max(128, shard // 2)), jnp.float32),
            pltpu.VMEM((slots, max(part, down_rows), max(up_cols, down_cols)), jnp.bfloat16),
            pltpu.SemaphoreType.DMA((slots,)),
            pltpu.SemaphoreType.DMA((2,)),
        ],
        compiler_params=pltpu.CompilerParams(vmem_limit_bytes=17 * MIB),
        cost_estimate=pl.CostEstimate(
            flops=4 * rows * depth * shard + 2 * rows * shard * (depth - width),
            bytes_accessed=4 * depth * shard,
            transcendentals=rows * shard,
        ),
        name="ffn",
    )(*panels, gate_weight, up_held, up_weight, down_weight)


def kept_kernel(hidden_ref, kept_ref, down_ref, out_ref, rest, sems):
    width = out_ref.shape[1]
    have, band = kept_ref.shape[1], rest.shape[2]
    me = lax.axis_index("hid")

    def copy(n):
        start = pl.multiple_of(me * width + have + n * band, 128)
        return pltpu.make_async_copy(
            down_ref.at[:, pl.ds(start, band)], rest.at[n], sems.at[n]
        )

    more = (width - have) // band
    for n in range(more):
        copy(n).start()

    @pl.loop(0, have // band)
    def _(n):
        columns = pl.ds(pl.multiple_of(n * band, 128), band)
        out_ref[:, columns] = jnp.dot(
            hidden_ref[...], kept_ref[:, columns], preferred_element_type=jnp.float32
        )

    @pl.loop(0, more)
    def _(n):
        copy(n).wait()
        columns = pl.ds(pl.multiple_of(have + n * band, 128), band)
        out_ref[:, columns] = jnp.dot(
            hidden_ref[...], rest[n], preferred_element_type=jnp.float32
        )


def kept_part(hidden, kept, down_weight):
    rows, shard = hidden.shape
    width = down_weight.shape[1] // lax.axis_size("hid")
    band = even(kept.shape[1], 512)
    more = max(1, (width - kept.shape[1]) // band)
    return pl.pallas_call(
        kept_kernel,
        out_shape=jax.ShapeDtypeStruct((rows, width), jnp.float32),
        in_specs=[IN_VMEM, IN_VMEM, ANYWHERE],
        out_specs=IN_VMEM,
        scratch_shapes=[
            pltpu.VMEM((more, shard, band), jnp.bfloat16),
            pltpu.SemaphoreType.DMA((more,)),
        ],
        compiler_params=pltpu.CompilerParams(vmem_limit_bytes=6 * MIB),
        cost_estimate=pl.CostEstimate(
            flops=2 * rows * shard * width, bytes_accessed=2 * shard * width, transcendentals=0
        ),
        name="kept_part",
    )(hidden, kept, down_weight)


def hid_sum_kernel(count, *refs):
    total = refs[0][...]
    for ref in refs[1:count]:
        total += ref[...].astype(jnp.float32)
    each = total.shape[0] // len(refs[count:])
    for step, ref in enumerate(refs[count:]):
        ref[...] = total[step * each : (step + 1) * each, :].astype(ref.dtype)


def hid_sum(parts, blocks):
    rows, width = parts[0].shape
    each = rows // blocks
    outs = [jax.ShapeDtypeStruct((each, width), jnp.float32)]
    outs += [jax.ShapeDtypeStruct((each, width), jnp.bfloat16)] * (blocks - 1)
    return pl.pallas_call(
        functools.partial(hid_sum_kernel, len(parts)),
        out_shape=tuple(outs),
        in_specs=[IN_VMEM] * len(parts),
        out_specs=(IN_VMEM,) * blocks,
        compiler_params=pltpu.CompilerParams(vmem_limit_bytes=4 * MIB),
        name="hid_sum",
    )(*parts)


def blk_sum_kernel(lanes, hids, *refs):
    *part_refs, out_ref = refs
    total = part_refs[0][...]
    for ref in part_refs[1:]:
        total += ref[...].astype(jnp.float32)
    rows = out_ref.shape[0]
    rounds = rows // lanes
    r = lax.broadcasted_iota(jnp.int32, (rows, rows), 0)
    c = lax.broadcasted_iota(jnp.int32, (rows, rows), 1)
    step = jnp.bitwise_xor(jnp.bitwise_and(r, lanes - 1), lax.axis_index("regroup"))
    turn = lax.shift_right_logical(step, log2(hids))
    core = jnp.bitwise_and(step, hids - 1)
    place = core * (lanes // hids) + turn
    order = (c == place * rounds + lax.shift_right_logical(r, log2(lanes))).astype(jnp.bfloat16)
    out_ref[...] = jnp.dot(
        order, total.astype(jnp.bfloat16), preferred_element_type=jnp.float32
    ).astype(jnp.bfloat16)


def blk_sum(parts):
    return pl.pallas_call(
        functools.partial(blk_sum_kernel, lax.axis_size("regroup"), lax.axis_size("hid")),
        out_shape=jax.ShapeDtypeStruct(parts[0].shape, jnp.bfloat16),
        in_specs=[IN_VMEM] * len(parts),
        out_specs=IN_VMEM,
        compiler_params=pltpu.CompilerParams(vmem_limit_bytes=4 * MIB),
        name="blk_sum",
    )(*parts)


def held(array):
    return pltpu.with_memory_space_constraint(array, pltpu.VMEM)


def on_device(tokens, kinds, slots, gains, gate_weight, up_weight, down_weight):
    blocks, lanes, hids = (lax.axis_size(axis) for axis in ("blk", "regroup", "hid"))
    tokens, kinds, slots, gains, up_weight, down_weight = (
        pltpu.with_memory_space_constraint(array, pltpu.HBM)
        for array in (tokens, kinds, slots, gains, up_weight, down_weight)
    )
    gate_weight = held(gate_weight)
    half = stacked(to_lanes(norm(tokens, kinds, slots, gains)))
    halves = [half] + [exchange(half, "blk", step) for step in range(1, blocks)]
    up_held = early(half, up_weight)
    for step in range(1, blocks):
        halves[step], up_held = lax.optimization_barrier((halves[step], up_held))
    panels = halves + [exchange(part, "hid", side) for side in range(1, hids) for part in halves]
    panels = [held(part) for part in panels]
    up_held = held(up_held)
    hidden, kept, *sent = ffn(panels, gate_weight, up_held, up_weight, down_weight, blocks)
    hidden, kept = held(hidden), held(kept)
    came = [exchange(part, "hid", step + 1) for step, part in enumerate(sent)]
    parts = hid_sum([kept_part(hidden, kept, down_weight)] + came, blocks)
    return blk_sum(
        [parts[0]] + [exchange(parts[step], "blk", step) for step in range(1, blocks)]
    )


def solution(mesh):
    placed = (
        P(("blk", "regroup"), None),
        P(("blk", "regroup")),
        P(("blk", "regroup"), None),
        P(),
        P(None, ("blk", "hid")),
        P(None, ("blk", "hid")),
        P(("blk", "hid"), None),
    )
    return jax.shard_map(
        on_device,
        mesh=mesh,
        in_specs=placed,
        out_specs=P(("blk", "regroup"), "hid"),
        check_vma=False,
    )
```

```python
import functools

import jax
import jax.numpy as jnp
from jax import lax
from jax.experimental import pallas as pl
from jax.experimental.pallas import tpu as pltpu
from jax.sharding import PartitionSpec as P

epsilon = 1e-05
MIB = 1 << 20

ANYWHERE = pl.BlockSpec(memory_space=pl.ANY)
IN_VMEM = pl.BlockSpec(memory_space=pltpu.VMEM)


def log2(number):
    bits = number.bit_length() - 1
    assert 1 << bits == number
    return bits


def exchange(array, axis, step):
    count = lax.axis_size(axis)
    log2(count)
    return lax.ppermute(array, axis, [(i, i ^ step) for i in range(count)])


def norm_kernel(lanes, hids, *refs):
    count = lanes // hids
    sources, piece_refs = refs[:4], refs[4 : 4 + count]
    targets, placed, sems = refs[4 + count : 8 + count], refs[8 + count], refs[9 + count]
    copies = [
        pltpu.make_async_copy(src, dst, sems.at[i])
        for i, (src, dst) in enumerate(zip(sources, targets))
    ]
    for copy in copies:
        copy.start()
    for copy in copies:
        copy.wait()
    tokens_ref, kinds_ref, slots_ref, gains_ref = targets
    rows = tokens_ref.shape[0]
    rounds = rows // lanes
    x = tokens_ref[...].astype(jnp.float32)
    row_scale = lax.rsqrt(jnp.mean(x * x, axis=1, keepdims=True) + epsilon)
    at = lax.broadcasted_iota(jnp.int32, (rows, 1), 0)
    kind = jnp.zeros((rows, 1), jnp.int32)
    for i in range(rows):
        kind = jnp.where(at == i, kinds_ref[i], kind)
    gain = jnp.broadcast_to(gains_ref[0:1, :], x.shape)
    for c in range(1, gains_ref.shape[0]):
        gain = jnp.where(kind == c, gains_ref[c : c + 1, :], gain)
    normed = (x * row_scale * gain).astype(jnp.bfloat16)
    target = lax.broadcasted_iota(jnp.int32, (count * rounds, rows), 0)
    turn = lax.shift_right_logical(target, log2(rounds))
    step = turn * hids + lax.axis_index("hid")
    lane = jnp.bitwise_xor(step, lax.axis_index("regroup"))
    slot = jnp.bitwise_and(target, rounds - 1) * lanes + lane
    placing = (jnp.broadcast_to(slots_ref[0:1, :], slot.shape) == slot).astype(jnp.bfloat16)
    placed[...] = jnp.dot(placing, normed, preferred_element_type=jnp.float32)
    for t, ref in enumerate(piece_refs):
        ref[...] = placed[t * rounds : (t + 1) * rounds, :].astype(jnp.bfloat16)


def norm(tokens, kinds, slots, gains):
    rows, features = tokens.shape
    lanes, hids = lax.axis_size("regroup"), lax.axis_size("hid")
    count, rounds = lanes // hids, rows // lanes
    return pl.pallas_call(
        functools.partial(norm_kernel, lanes, hids),
        out_shape=(jax.ShapeDtypeStruct((rounds, features), jnp.bfloat16),) * count,
        in_specs=[ANYWHERE] * 4,
        out_specs=(IN_VMEM,) * count,
        scratch_shapes=[
            pltpu.VMEM(tokens.shape, tokens.dtype),
            pltpu.SMEM(kinds.shape, kinds.dtype),
            pltpu.VMEM(slots.shape, slots.dtype),
            pltpu.VMEM(gains.shape, gains.dtype),
            pltpu.VMEM((count * rounds, features), jnp.float32),
            pltpu.SemaphoreType.DMA((4,)),
        ],
        compiler_params=pltpu.CompilerParams(vmem_limit_bytes=4 * MIB),
        cost_estimate=pl.CostEstimate(flops=0, bytes_accessed=48 * MIB, transcendentals=0),
        name="norm",
    )(tokens, kinds, slots, gains)


def to_lanes(pieces):
    lanes, hids = lax.axis_size("regroup"), lax.axis_size("hid")
    count = len(pieces)
    assert count * hids == lanes

    def pairs(t):
        for lane in range(lanes):
            for core in range(hids):
                yield lane * hids + core, (lane ^ (t * hids + core)) * hids + core

    return [lax.ppermute(piece, ("regroup", "hid"), list(pairs(t))) for t, piece in enumerate(pieces)]


def stack_kernel(*refs):
    *piece_refs, out_ref, stack = refs
    rounds = piece_refs[0].shape[0]
    for t, ref in enumerate(piece_refs):
        stack[t * rounds : (t + 1) * rounds, :] = ref[...].astype(jnp.float32)
    out_ref[...] = stack[...].astype(jnp.bfloat16)


def stacked(pieces):
    rounds, width = pieces[0].shape
    rows = len(pieces) * rounds
    return pl.pallas_call(
        stack_kernel,
        out_shape=jax.ShapeDtypeStruct((rows, width), jnp.bfloat16),
        in_specs=[IN_VMEM] * len(pieces),
        out_specs=IN_VMEM,
        scratch_shapes=[pltpu.VMEM((rows, width), jnp.float32)],
        compiler_params=pltpu.CompilerParams(vmem_limit_bytes=4 * MIB),
        name="stacked",
    )(*pieces)


def twice(count):
    return 1 if count % 2 else 2


def even(total, most):
    return next(size for size in range(min(most, total), 0, -128) if total % size == 0)


def early_kernel(width, after_ref, up_ref, out_ref, sem):
    start = pl.multiple_of(lax.axis_index("hid") * width, width)
    copy = pltpu.make_async_copy(up_ref.at[pl.ds(start, out_ref.shape[0]), :], out_ref, sem)
    copy.start()
    copy.wait()


def early(after, up_weight):
    width = up_weight.shape[0] // lax.axis_size("hid")
    depth = width - even(width, 1024)
    shard = up_weight.shape[1]
    return pl.pallas_call(
        functools.partial(early_kernel, width),
        out_shape=pltpu.VMEM((depth, shard), jnp.bfloat16),
        in_specs=[ANYWHERE, ANYWHERE],
        out_specs=IN_VMEM,
        scratch_shapes=[pltpu.SemaphoreType.DMA(())],
        compiler_params=pltpu.CompilerParams(vmem_limit_bytes=1 * MIB),
        cost_estimate=pl.CostEstimate(
            flops=0, bytes_accessed=2 * depth * shard, transcendentals=0
        ),
        name="early",
    )(after, up_weight)


def ffn_kernel(blocks, hids, plan, *refs):
    slots, part, up_cols, down_rows, down_cols = plan
    count = blocks * hids
    panel_refs = refs[:count]
    gate_ref, held_ref, up_ref, down_ref = refs[count : count + 4]
    hidden_ref, kept = refs[count + 4 : count + 6]
    out_refs = refs[count + 6 : count + 5 + hids]
    panel, up_sum, act, ring, ring_sems, kept_sems = refs[count + 5 + hids :]
    rows, depth = panel.shape
    each = rows // blocks
    shard = gate_ref.shape[1]
    width = depth // hids
    me = lax.axis_index("hid")
    inside, across = width // part, shard // up_cols
    deep, wide = shard // down_rows, width // down_cols
    skip = held_ref.shape[0] // part
    up_count = (hids * inside - skip) * across
    down_count = (hids - 1) * wide * deep

    def side_start(side):
        return jnp.bitwise_xor(me, side) * width

    def up_copy(n):
        u, c = n // across + skip, n % across
        side, p = u // inside, u % inside
        return pltpu.make_async_copy(
            up_ref.at[
                pl.ds(pl.multiple_of(side_start(side) + p * part, part), part),
                pl.ds(pl.multiple_of(c * up_cols, up_cols), up_cols),
            ],
            ring.at[n % slots, pl.ds(0, part), pl.ds(0, up_cols)],
            ring_sems.at[n % slots],
        )

    def down_copy(n):
        side, c, k = n // (wide * deep) + 1, n // deep % wide, n % deep
        slot = (n + up_count) % slots
        return pltpu.make_async_copy(
            down_ref.at[
                pl.ds(pl.multiple_of(k * down_rows, down_rows), down_rows),
                pl.ds(pl.multiple_of(side_start(side) + c * down_cols, 128), down_cols),
            ],
            ring.at[slot, pl.ds(0, down_rows), pl.ds(0, down_cols)],
            ring_sems.at[slot],
        )

    def kept_copy(n):
        size = kept.shape[1] // 2
        start = pl.multiple_of(me * width + n * size, 128)
        return pltpu.make_async_copy(
            down_ref.at[:, pl.ds(start, size)],
            kept.at[:, n * size : (n + 1) * size],
            kept_sems.at[n],
        )

    def start_next(n):
        if isinstance(n, int):
            if n < up_count:
                up_copy(n).start()
            elif n < up_count + down_count:
                down_copy(n - up_count).start()
            return

        @pl.when(n < up_count)
        def _():
            up_copy(n).start()

        @pl.when((n >= up_count) & (n < up_count + down_count))
        def _():
            down_copy(n - up_count).start()

    for n in range(slots):
        start_next(n)
    kept_copy(0).start()
    for step in range(blocks):
        sides = [
            panel_refs[side * blocks + step][...].astype(jnp.float32) for side in range(hids)
        ]
        panel[step * each : (step + 1) * each, :] = jnp.concatenate(sides, axis=0).astype(
            jnp.bfloat16
        )
    chunk = even(shard, 1024)
    own = pl.ds(pl.multiple_of(me * width, width), skip * part)

    @pl.loop(0, shard // chunk)
    def _(c):
        columns = pl.ds(pl.multiple_of(c * chunk, chunk), chunk)
        up_sum[:, columns] = jnp.dot(
            panel[:, own], held_ref[:, columns], preferred_element_type=jnp.float32
        )

    def gate_act(columns):
        gate = jnp.dot(panel[...], gate_ref[:, columns], preferred_element_type=jnp.float32)
        return gate / (1.0 + jnp.exp(-gate))

    before = shard // chunk // 2

    @pl.loop(0, before)
    def _(c):
        columns = pl.ds(pl.multiple_of(c * chunk, chunk), chunk)
        act[:, columns] = gate_act(columns)

    @pl.loop(skip, hids * inside, unroll=twice(hids * inside - skip))
    def _(u):
        side, p = u // inside, u % inside
        x = panel[:, pl.ds(pl.multiple_of(side_start(side) + p * part, part), part)]
        for c in range(across):
            n = (u - skip) * across + c
            up_copy(n).wait()
            columns = slice(c * up_cols, (c + 1) * up_cols)
            up_sum[:, columns] += jnp.dot(
                x,
                ring[n % slots, 0:part, 0:up_cols],
                preferred_element_type=jnp.float32,
            )
            start_next(n + slots)

    kept_copy(1).start()

    @pl.loop(before, shard // chunk)
    def _(c):
        columns = pl.ds(pl.multiple_of(c * chunk, chunk), chunk)
        hidden_ref[:, columns] = (gate_act(columns) * up_sum[:, columns]).astype(jnp.bfloat16)

    done = slice(0, before * chunk)
    if before:
        hidden_ref[:, done] = (act[:, done] * up_sum[:, done]).astype(jnp.bfloat16)

    for side in range(1, hids):

        @pl.loop(0, wide)
        def _(c):
            total = None
            for k in range(deep):
                down_copy(((side - 1) * wide + c) * deep + k).wait()
            for k in range(deep):
                n = ((side - 1) * wide + c) * deep + k
                value = jnp.dot(
                    hidden_ref[:, k * down_rows : (k + 1) * down_rows],
                    ring[(n + up_count) % slots, 0:down_rows, 0:down_cols],
                    preferred_element_type=jnp.float32,
                )
                total = value if total is None else total + value
            for k in range(deep):
                start_next(((side - 1) * wide + c) * deep + k + up_count + slots)
            columns = pl.ds(pl.multiple_of(c * down_cols, 128), down_cols)
            out_refs[side - 1][:, columns] = total.astype(jnp.bfloat16)

    for n in range(2):
        kept_copy(n).wait()


def ffn(panels, gate_weight, up_held, up_weight, down_weight, blocks):
    hids = lax.axis_size("hid")
    each, depth = panels[0].shape
    rows, width = blocks * hids * each, depth // hids
    shard = gate_weight.shape[1]
    part, up_cols = even(width, 1024), even(shard, 1024)
    down_rows, down_cols = even(shard, 1024), even(width, 1024)
    slots = 6
    outs = [
        pltpu.VMEM((rows, shard), jnp.bfloat16),
        pltpu.VMEM((shard, (width // down_cols + 1) // 2 * down_cols), jnp.bfloat16),
    ] + [pltpu.VMEM((rows, width), jnp.bfloat16)] * (hids - 1)
    return pl.pallas_call(
        functools.partial(
            ffn_kernel, blocks, hids, (slots, part, up_cols, down_rows, down_cols)
        ),
        out_shape=tuple(outs),
        in_specs=[IN_VMEM] * (len(panels) + 2) + [ANYWHERE, ANYWHERE],
        out_specs=(IN_VMEM,) * (1 + hids),
        scratch_shapes=[
            pltpu.VMEM((rows, depth), jnp.bfloat16),
            pltpu.VMEM((rows, shard), jnp.float32),
            pltpu.VMEM((rows, max(128, shard // 2)), jnp.float32),
            pltpu.VMEM((slots, max(part, down_rows), max(up_cols, down_cols)), jnp.bfloat16),
            pltpu.SemaphoreType.DMA((slots,)),
            pltpu.SemaphoreType.DMA((2,)),
        ],
        compiler_params=pltpu.CompilerParams(vmem_limit_bytes=17 * MIB),
        cost_estimate=pl.CostEstimate(
            flops=4 * rows * depth * shard + 2 * rows * shard * (depth - width),
            bytes_accessed=4 * depth * shard,
            transcendentals=rows * shard,
        ),
        name="ffn",
    )(*panels, gate_weight, up_held, up_weight, down_weight)


def kept_kernel(hidden_ref, kept_ref, down_ref, out_ref, rest, sems):
    width = out_ref.shape[1]
    have, band = kept_ref.shape[1], rest.shape[2]
    me = lax.axis_index("hid")

    def copy(n):
        start = pl.multiple_of(me * width + have + n * band, 128)
        return pltpu.make_async_copy(
            down_ref.at[:, pl.ds(start, band)], rest.at[n], sems.at[n]
        )

    more = (width - have) // band
    for n in range(more):
        copy(n).start()

    @pl.loop(0, have // band, unroll=twice(have // band))
    def _(n):
        columns = pl.ds(pl.multiple_of(n * band, 128), band)
        out_ref[:, columns] = jnp.dot(
            hidden_ref[...], kept_ref[:, columns], preferred_element_type=jnp.float32
        )

    @pl.loop(0, more)
    def _(n):
        copy(n).wait()
        columns = pl.ds(pl.multiple_of(have + n * band, 128), band)
        out_ref[:, columns] = jnp.dot(
            hidden_ref[...], rest[n], preferred_element_type=jnp.float32
        )


def kept_part(hidden, kept, down_weight):
    rows, shard = hidden.shape
    width = down_weight.shape[1] // lax.axis_size("hid")
    band = even(kept.shape[1], 512)
    more = max(1, (width - kept.shape[1]) // band)
    return pl.pallas_call(
        kept_kernel,
        out_shape=jax.ShapeDtypeStruct((rows, width), jnp.float32),
        in_specs=[IN_VMEM, IN_VMEM, ANYWHERE],
        out_specs=IN_VMEM,
        scratch_shapes=[
            pltpu.VMEM((more, shard, band), jnp.bfloat16),
            pltpu.SemaphoreType.DMA((more,)),
        ],
        compiler_params=pltpu.CompilerParams(vmem_limit_bytes=6 * MIB),
        cost_estimate=pl.CostEstimate(
            flops=2 * rows * shard * width, bytes_accessed=2 * shard * width, transcendentals=0
        ),
        name="kept_part",
    )(hidden, kept, down_weight)


def hid_sum_kernel(hids, *refs):
    parts = [ref[...].astype(jnp.float32) for ref in refs[:hids]]
    each = parts[0].shape[0] // len(refs[hids:])
    size = each // hids
    for step, ref in enumerate(refs[hids:]):
        lined = []
        for side in range(hids):
            total = None
            for q, part in enumerate(parts):
                start = step * each + (side ^ q) * size
                value = part[start : start + size, :]
                total = value if total is None else total + value
            lined.append(total)
        ref[...] = jnp.concatenate(lined, axis=0).astype(ref.dtype)


def hid_sum(parts, blocks):
    rows, width = parts[0].shape
    each = rows // blocks
    outs = [jax.ShapeDtypeStruct((each, width), jnp.float32)]
    outs += [jax.ShapeDtypeStruct((each, width), jnp.bfloat16)] * (blocks - 1)
    return pl.pallas_call(
        functools.partial(hid_sum_kernel, len(parts)),
        out_shape=tuple(outs),
        in_specs=[IN_VMEM] * len(parts),
        out_specs=(IN_VMEM,) * blocks,
        compiler_params=pltpu.CompilerParams(vmem_limit_bytes=4 * MIB),
        name="hid_sum",
    )(*parts)


def blk_sum_kernel(lanes, hids, *refs):
    *part_refs, out_ref = refs
    total = part_refs[0][...]
    for ref in part_refs[1:]:
        total += ref[...].astype(jnp.float32)
    rows = out_ref.shape[0]
    rounds = rows // lanes
    r = lax.broadcasted_iota(jnp.int32, (rows, rows), 0)
    c = lax.broadcasted_iota(jnp.int32, (rows, rows), 1)
    step = jnp.bitwise_xor(jnp.bitwise_and(r, lanes - 1), lax.axis_index("regroup"))
    turn = lax.shift_right_logical(step, log2(hids))
    side = jnp.bitwise_xor(jnp.bitwise_and(step, hids - 1), lax.axis_index("hid"))
    place = side * (lanes // hids) + turn
    order = (c == place * rounds + lax.shift_right_logical(r, log2(lanes))).astype(jnp.bfloat16)
    out_ref[...] = jnp.dot(
        order, total.astype(jnp.bfloat16), preferred_element_type=jnp.float32
    ).astype(jnp.bfloat16)


def blk_sum(parts):
    return pl.pallas_call(
        functools.partial(blk_sum_kernel, lax.axis_size("regroup"), lax.axis_size("hid")),
        out_shape=jax.ShapeDtypeStruct(parts[0].shape, jnp.bfloat16),
        in_specs=[IN_VMEM] * len(parts),
        out_specs=IN_VMEM,
        compiler_params=pltpu.CompilerParams(vmem_limit_bytes=4 * MIB),
        name="blk_sum",
    )(*parts)


def held(array):
    return pltpu.with_memory_space_constraint(array, pltpu.VMEM)


def on_device(tokens, kinds, slots, gains, gate_weight, up_weight, down_weight):
    blocks, lanes, hids = (lax.axis_size(axis) for axis in ("blk", "regroup", "hid"))
    tokens, kinds, slots, gains, up_weight, down_weight = (
        pltpu.with_memory_space_constraint(array, pltpu.HBM)
        for array in (tokens, kinds, slots, gains, up_weight, down_weight)
    )
    gate_weight = held(gate_weight)
    half = stacked(to_lanes(norm(tokens, kinds, slots, gains)))
    halves = [half] + [exchange(half, "blk", step) for step in range(1, blocks)]
    up_held = early(half, up_weight)
    for step in range(1, blocks):
        halves[step], up_held = lax.optimization_barrier((halves[step], up_held))
    panels = halves + [exchange(part, "hid", side) for side in range(1, hids) for part in halves]
    panels = [held(part) for part in panels]
    up_held = held(up_held)
    hidden, kept, *sent = ffn(panels, gate_weight, up_held, up_weight, down_weight, blocks)
    hidden, kept = held(hidden), held(kept)
    came = [exchange(part, "hid", step + 1) for step, part in enumerate(sent)]
    parts = hid_sum([kept_part(hidden, kept, down_weight)] + came, blocks)
    return blk_sum(
        [parts[0]] + [exchange(parts[step], "blk", step) for step in range(1, blocks)]
    )


def solution(mesh):
    placed = (
        P(("blk", "regroup"), None),
        P(("blk", "regroup")),
        P(("blk", "regroup"), None),
        P(),
        P(None, ("blk", "hid")),
        P(None, ("blk", "hid")),
        P(("blk", "hid"), None),
    )
    return jax.shard_map(
        on_device,
        mesh=mesh,
        in_specs=placed,
        out_specs=P(("blk", "regroup"), "hid"),
        check_vma=False,
    )
```

```python
import functools

import jax
import jax.numpy as jnp
from jax import lax
from jax.experimental import pallas as pl
from jax.experimental.pallas import tpu as pltpu
from jax.sharding import PartitionSpec as P

epsilon = 1e-05
MIB = 1 << 20

ANYWHERE = pl.BlockSpec(memory_space=pl.ANY)
IN_VMEM = pl.BlockSpec(memory_space=pltpu.VMEM)


def log2(number):
    bits = number.bit_length() - 1
    assert 1 << bits == number
    return bits


def exchange(array, axis, step):
    count = lax.axis_size(axis)
    log2(count)
    return lax.ppermute(array, axis, [(i, i ^ step) for i in range(count)])


def norm_kernel(lanes, hids, *refs):
    count = lanes // hids
    sources, piece_refs = refs[:4], refs[4 : 4 + count]
    targets, placed, sems = refs[4 + count : 8 + count], refs[8 + count], refs[9 + count]
    copies = [
        pltpu.make_async_copy(src, dst, sems.at[i])
        for i, (src, dst) in enumerate(zip(sources, targets))
    ]
    for copy in copies:
        copy.start()
    for copy in copies:
        copy.wait()
    tokens_ref, kinds_ref, slots_ref, gains_ref = targets
    rows = tokens_ref.shape[0]
    rounds = rows // lanes
    x = tokens_ref[...].astype(jnp.float32)
    row_scale = lax.rsqrt(jnp.mean(x * x, axis=1, keepdims=True) + epsilon)
    at = lax.broadcasted_iota(jnp.int32, (rows, 1), 0)
    kind = jnp.zeros((rows, 1), jnp.int32)
    for i in range(rows):
        kind = jnp.where(at == i, kinds_ref[i], kind)
    gain = jnp.broadcast_to(gains_ref[0:1, :], x.shape)
    for c in range(1, gains_ref.shape[0]):
        gain = jnp.where(kind == c, gains_ref[c : c + 1, :], gain)
    normed = (x * row_scale * gain).astype(jnp.bfloat16)
    target = lax.broadcasted_iota(jnp.int32, (count * rounds, rows), 0)
    turn = lax.shift_right_logical(target, log2(rounds))
    step = turn * hids + lax.axis_index("hid")
    lane = jnp.bitwise_xor(step, lax.axis_index("regroup"))
    slot = jnp.bitwise_and(target, rounds - 1) * lanes + lane
    placing = (jnp.broadcast_to(slots_ref[0:1, :], slot.shape) == slot).astype(jnp.bfloat16)
    placed[...] = jnp.dot(placing, normed, preferred_element_type=jnp.float32)
    for t, ref in enumerate(piece_refs):
        ref[...] = placed[t * rounds : (t + 1) * rounds, :].astype(jnp.bfloat16)


def norm(tokens, kinds, slots, gains):
    rows, features = tokens.shape
    lanes, hids = lax.axis_size("regroup"), lax.axis_size("hid")
    count, rounds = lanes // hids, rows // lanes
    return pl.pallas_call(
        functools.partial(norm_kernel, lanes, hids),
        out_shape=(jax.ShapeDtypeStruct((rounds, features), jnp.bfloat16),) * count,
        in_specs=[ANYWHERE] * 4,
        out_specs=(IN_VMEM,) * count,
        scratch_shapes=[
            pltpu.VMEM(tokens.shape, tokens.dtype),
            pltpu.SMEM(kinds.shape, kinds.dtype),
            pltpu.VMEM(slots.shape, slots.dtype),
            pltpu.VMEM(gains.shape, gains.dtype),
            pltpu.VMEM((count * rounds, features), jnp.float32),
            pltpu.SemaphoreType.DMA((4,)),
        ],
        compiler_params=pltpu.CompilerParams(vmem_limit_bytes=4 * MIB),
        cost_estimate=pl.CostEstimate(flops=0, bytes_accessed=48 * MIB, transcendentals=0),
        name="norm",
    )(tokens, kinds, slots, gains)


def to_lanes(pieces):
    lanes, hids = lax.axis_size("regroup"), lax.axis_size("hid")
    count = len(pieces)
    assert count * hids == lanes

    def pairs(t):
        for lane in range(lanes):
            for core in range(hids):
                yield lane * hids + core, (lane ^ (t * hids + core)) * hids + core

    far = {t: lax.ppermute(pieces[t], ("regroup", "hid"), list(pairs(t))) for t in reversed(range(count))}
    return [far[t] for t in range(count)]


def stack_kernel(*refs):
    *piece_refs, out_ref, stack = refs
    rounds = piece_refs[0].shape[0]
    for t, ref in enumerate(piece_refs):
        stack[t * rounds : (t + 1) * rounds, :] = ref[...].astype(jnp.float32)
    out_ref[...] = stack[...].astype(jnp.bfloat16)


def stacked(pieces):
    rounds, width = pieces[0].shape
    rows = len(pieces) * rounds
    return pl.pallas_call(
        stack_kernel,
        out_shape=jax.ShapeDtypeStruct((rows, width), jnp.bfloat16),
        in_specs=[IN_VMEM] * len(pieces),
        out_specs=IN_VMEM,
        scratch_shapes=[pltpu.VMEM((rows, width), jnp.float32)],
        compiler_params=pltpu.CompilerParams(vmem_limit_bytes=4 * MIB),
        name="stacked",
    )(*pieces)


def twice(count):
    return 1 if count % 2 else 2


def even(total, most):
    return next(size for size in range(min(most, total), 0, -128) if total % size == 0)


def early_kernel(width, after_ref, up_ref, out_ref, sem):
    start = pl.multiple_of(lax.axis_index("hid") * width, width)
    copy = pltpu.make_async_copy(up_ref.at[pl.ds(start, out_ref.shape[0]), :], out_ref, sem)
    copy.start()
    copy.wait()


def early(after, up_weight):
    width = up_weight.shape[0] // lax.axis_size("hid")
    depth = width - even(width, 1024)
    shard = up_weight.shape[1]
    return pl.pallas_call(
        functools.partial(early_kernel, width),
        out_shape=pltpu.VMEM((depth, shard), jnp.bfloat16),
        in_specs=[ANYWHERE, ANYWHERE],
        out_specs=IN_VMEM,
        scratch_shapes=[pltpu.SemaphoreType.DMA(())],
        compiler_params=pltpu.CompilerParams(vmem_limit_bytes=1 * MIB),
        cost_estimate=pl.CostEstimate(
            flops=0, bytes_accessed=2 * depth * shard, transcendentals=0
        ),
        name="early",
    )(after, up_weight)


def ffn_kernel(blocks, hids, plan, *refs):
    slots, part, up_cols, down_rows, down_cols = plan
    count = blocks * hids
    panel_refs = refs[:count]
    gate_ref, held_ref, up_ref, down_ref = refs[count : count + 4]
    hidden_ref, kept = refs[count + 4 : count + 6]
    out_refs = refs[count + 6 : count + 5 + hids]
    panel, up_sum, act, ring, ring_sems, kept_sems = refs[count + 5 + hids :]
    rows, depth = panel.shape
    each = rows // blocks
    shard = gate_ref.shape[1]
    width = depth // hids
    me = lax.axis_index("hid")
    inside, across = width // part, shard // up_cols
    deep, wide = shard // down_rows, width // down_cols
    skip = held_ref.shape[0] // part
    up_count = (hids * inside - skip) * across
    down_count = (hids - 1) * wide * deep

    def side_start(side):
        return jnp.bitwise_xor(me, side) * width

    def up_copy(n):
        u, c = n // across + skip, n % across
        side, p = u // inside, u % inside
        return pltpu.make_async_copy(
            up_ref.at[
                pl.ds(pl.multiple_of(side_start(side) + p * part, part), part),
                pl.ds(pl.multiple_of(c * up_cols, up_cols), up_cols),
            ],
            ring.at[n % slots, pl.ds(0, part), pl.ds(0, up_cols)],
            ring_sems.at[n % slots],
        )

    def down_copy(n):
        side, c, k = n // (wide * deep) + 1, n // deep % wide, n % deep
        slot = (n + up_count) % slots
        return pltpu.make_async_copy(
            down_ref.at[
                pl.ds(pl.multiple_of(k * down_rows, down_rows), down_rows),
                pl.ds(pl.multiple_of(side_start(side) + c * down_cols, 128), down_cols),
            ],
            ring.at[slot, pl.ds(0, down_rows), pl.ds(0, down_cols)],
            ring_sems.at[slot],
        )

    def kept_copy(n):
        size = kept.shape[1] // 2
        start = pl.multiple_of(me * width + n * size, 128)
        return pltpu.make_async_copy(
            down_ref.at[:, pl.ds(start, size)],
            kept.at[:, n * size : (n + 1) * size],
            kept_sems.at[n],
        )

    def start_next(n):
        if isinstance(n, int):
            if n < up_count:
                up_copy(n).start()
            elif n < up_count + down_count:
                down_copy(n - up_count).start()
            return

        @pl.when(n < up_count)
        def _():
            up_copy(n).start()

        @pl.when((n >= up_count) & (n < up_count + down_count))
        def _():
            down_copy(n - up_count).start()

    for n in range(slots):
        start_next(n)
    kept_copy(0).start()
    for step in range(blocks):
        sides = [
            panel_refs[side * blocks + step][...].astype(jnp.float32) for side in range(hids)
        ]
        panel[step * each : (step + 1) * each, :] = jnp.concatenate(sides, axis=0).astype(
            jnp.bfloat16
        )
    chunk = even(shard, 1024)
    own = pl.ds(pl.multiple_of(me * width, width), skip * part)

    @pl.loop(0, shard // chunk)
    def _(c):
        columns = pl.ds(pl.multiple_of(c * chunk, chunk), chunk)
        up_sum[:, columns] = jnp.dot(
            panel[:, own], held_ref[:, columns], preferred_element_type=jnp.float32
        )

    def gate_act(columns):
        gate = jnp.dot(panel[...], gate_ref[:, columns], preferred_element_type=jnp.float32)
        return gate / (1.0 + jnp.exp(-gate))

    before = shard // chunk // 2

    @pl.loop(0, before)
    def _(c):
        columns = pl.ds(pl.multiple_of(c * chunk, chunk), chunk)
        act[:, columns] = gate_act(columns)

    @pl.loop(skip, hids * inside, unroll=twice(hids * inside - skip))
    def _(u):
        side, p = u // inside, u % inside
        x = panel[:, pl.ds(pl.multiple_of(side_start(side) + p * part, part), part)]
        for c in range(across):
            n = (u - skip) * across + c
            up_copy(n).wait()
            columns = slice(c * up_cols, (c + 1) * up_cols)
            up_sum[:, columns] += jnp.dot(
                x,
                ring[n % slots, 0:part, 0:up_cols],
                preferred_element_type=jnp.float32,
            )
            start_next(n + slots)

    kept_copy(1).start()

    @pl.loop(before, shard // chunk)
    def _(c):
        columns = pl.ds(pl.multiple_of(c * chunk, chunk), chunk)
        hidden_ref[:, columns] = (gate_act(columns) * up_sum[:, columns]).astype(jnp.bfloat16)

    done = slice(0, before * chunk)
    if before:
        hidden_ref[:, done] = (act[:, done] * up_sum[:, done]).astype(jnp.bfloat16)

    for side in range(1, hids):

        @pl.loop(0, wide, unroll=wide)
        def _(c):
            total = None
            for k in range(deep):
                down_copy(((side - 1) * wide + c) * deep + k).wait()
            for k in range(deep):
                n = ((side - 1) * wide + c) * deep + k
                value = jnp.dot(
                    hidden_ref[:, k * down_rows : (k + 1) * down_rows],
                    ring[(n + up_count) % slots, 0:down_rows, 0:down_cols],
                    preferred_element_type=jnp.float32,
                )
                total = value if total is None else total + value
            for k in range(deep):
                start_next(((side - 1) * wide + c) * deep + k + up_count + slots)
            columns = pl.ds(pl.multiple_of(c * down_cols, 128), down_cols)
            out_refs[side - 1][:, columns] = total.astype(jnp.bfloat16)

    for n in range(2):
        kept_copy(n).wait()


def ffn(panels, gate_weight, up_held, up_weight, down_weight, blocks):
    hids = lax.axis_size("hid")
    each, depth = panels[0].shape
    rows, width = blocks * hids * each, depth // hids
    shard = gate_weight.shape[1]
    part, up_cols = even(width, 1024), even(shard, 1024)
    down_rows, down_cols = even(shard, 1024), even(width, 1024)
    slots = 6
    outs = [
        pltpu.VMEM((rows, shard), jnp.bfloat16),
        pltpu.VMEM((shard, (width // down_cols + 1) // 2 * down_cols), jnp.bfloat16),
    ] + [pltpu.VMEM((rows, width), jnp.bfloat16)] * (hids - 1)
    return pl.pallas_call(
        functools.partial(
            ffn_kernel, blocks, hids, (slots, part, up_cols, down_rows, down_cols)
        ),
        out_shape=tuple(outs),
        in_specs=[IN_VMEM] * (len(panels) + 2) + [ANYWHERE, ANYWHERE],
        out_specs=(IN_VMEM,) * (1 + hids),
        scratch_shapes=[
            pltpu.VMEM((rows, depth), jnp.bfloat16),
            pltpu.VMEM((rows, shard), jnp.float32),
            pltpu.VMEM((rows, max(128, shard // 2)), jnp.float32),
            pltpu.VMEM((slots, max(part, down_rows), max(up_cols, down_cols)), jnp.bfloat16),
            pltpu.SemaphoreType.DMA((slots,)),
            pltpu.SemaphoreType.DMA((2,)),
        ],
        compiler_params=pltpu.CompilerParams(vmem_limit_bytes=17 * MIB),
        cost_estimate=pl.CostEstimate(
            flops=4 * rows * depth * shard + 2 * rows * shard * (depth - width),
            bytes_accessed=4 * depth * shard,
            transcendentals=rows * shard,
        ),
        name="ffn",
    )(*panels, gate_weight, up_held, up_weight, down_weight)


def kept_kernel(hidden_ref, kept_ref, down_ref, out_ref, rest, sems):
    width = out_ref.shape[1]
    have, band = kept_ref.shape[1], rest.shape[2]
    me = lax.axis_index("hid")

    def copy(n):
        start = pl.multiple_of(me * width + have + n * band, 128)
        return pltpu.make_async_copy(
            down_ref.at[:, pl.ds(start, band)], rest.at[n], sems.at[n]
        )

    more = (width - have) // band
    for n in range(more):
        copy(n).start()

    @pl.loop(0, have // band, unroll=twice(have // band))
    def _(n):
        columns = pl.ds(pl.multiple_of(n * band, 128), band)
        out_ref[:, columns] = jnp.dot(
            hidden_ref[...], kept_ref[:, columns], preferred_element_type=jnp.float32
        )

    @pl.loop(0, more)
    def _(n):
        copy(n).wait()
        columns = pl.ds(pl.multiple_of(have + n * band, 128), band)
        out_ref[:, columns] = jnp.dot(
            hidden_ref[...], rest[n], preferred_element_type=jnp.float32
        )


def kept_part(hidden, kept, down_weight):
    rows, shard = hidden.shape
    width = down_weight.shape[1] // lax.axis_size("hid")
    band = even(kept.shape[1], 512)
    more = max(1, (width - kept.shape[1]) // band)
    return pl.pallas_call(
        kept_kernel,
        out_shape=jax.ShapeDtypeStruct((rows, width), jnp.float32),
        in_specs=[IN_VMEM, IN_VMEM, ANYWHERE],
        out_specs=IN_VMEM,
        scratch_shapes=[
            pltpu.VMEM((more, shard, band), jnp.bfloat16),
            pltpu.SemaphoreType.DMA((more,)),
        ],
        compiler_params=pltpu.CompilerParams(vmem_limit_bytes=6 * MIB),
        cost_estimate=pl.CostEstimate(
            flops=2 * rows * shard * width, bytes_accessed=2 * shard * width, transcendentals=0
        ),
        name="kept_part",
    )(hidden, kept, down_weight)


def hid_sum_kernel(hids, *refs):
    parts = [ref[...].astype(jnp.float32) for ref in refs[:hids]]
    each = parts[0].shape[0] // len(refs[hids:])
    size = each // hids
    for step, ref in enumerate(refs[hids:]):
        lined = []
        for side in range(hids):
            total = None
            for q, part in enumerate(parts):
                start = step * each + (side ^ q) * size
                value = part[start : start + size, :]
                total = value if total is None else total + value
            lined.append(total)
        ref[...] = jnp.concatenate(lined, axis=0).astype(ref.dtype)


def hid_sum(parts, blocks):
    rows, width = parts[0].shape
    each = rows // blocks
    outs = [jax.ShapeDtypeStruct((each, width), jnp.float32)]
    outs += [jax.ShapeDtypeStruct((each, width), jnp.bfloat16)] * (blocks - 1)
    return pl.pallas_call(
        functools.partial(hid_sum_kernel, len(parts)),
        out_shape=tuple(outs),
        in_specs=[IN_VMEM] * len(parts),
        out_specs=(IN_VMEM,) * blocks,
        compiler_params=pltpu.CompilerParams(vmem_limit_bytes=4 * MIB),
        name="hid_sum",
    )(*parts)


def blk_sum_kernel(lanes, hids, *refs):
    *part_refs, out_ref = refs
    total = part_refs[0][...]
    for ref in part_refs[1:]:
        total += ref[...].astype(jnp.float32)
    rows = out_ref.shape[0]
    rounds = rows // lanes
    r = lax.broadcasted_iota(jnp.int32, (rows, rows), 0)
    c = lax.broadcasted_iota(jnp.int32, (rows, rows), 1)
    step = jnp.bitwise_xor(jnp.bitwise_and(r, lanes - 1), lax.axis_index("regroup"))
    turn = lax.shift_right_logical(step, log2(hids))
    side = jnp.bitwise_xor(jnp.bitwise_and(step, hids - 1), lax.axis_index("hid"))
    place = side * (lanes // hids) + turn
    order = (c == place * rounds + lax.shift_right_logical(r, log2(lanes))).astype(jnp.bfloat16)
    out_ref[...] = jnp.dot(
        order, total.astype(jnp.bfloat16), preferred_element_type=jnp.float32
    ).astype(jnp.bfloat16)


def blk_sum(parts):
    return pl.pallas_call(
        functools.partial(blk_sum_kernel, lax.axis_size("regroup"), lax.axis_size("hid")),
        out_shape=jax.ShapeDtypeStruct(parts[0].shape, jnp.bfloat16),
        in_specs=[IN_VMEM] * len(parts),
        out_specs=IN_VMEM,
        compiler_params=pltpu.CompilerParams(vmem_limit_bytes=4 * MIB),
        name="blk_sum",
    )(*parts)


def held(array):
    return pltpu.with_memory_space_constraint(array, pltpu.VMEM)


def on_device(tokens, kinds, slots, gains, gate_weight, up_weight, down_weight):
    blocks, lanes, hids = (lax.axis_size(axis) for axis in ("blk", "regroup", "hid"))
    tokens, kinds, slots, gains, up_weight, down_weight = (
        pltpu.with_memory_space_constraint(array, pltpu.HBM)
        for array in (tokens, kinds, slots, gains, up_weight, down_weight)
    )
    gate_weight = held(gate_weight)
    half = stacked(to_lanes(norm(tokens, kinds, slots, gains)))
    halves = [half] + [exchange(half, "blk", step) for step in range(1, blocks)]
    up_held = early(half, up_weight)
    for step in range(1, blocks):
        halves[step], up_held = lax.optimization_barrier((halves[step], up_held))
    panels = halves + [exchange(part, "hid", side) for side in range(1, hids) for part in halves]
    panels = [held(part) for part in panels]
    up_held = held(up_held)
    hidden, kept, *sent = ffn(panels, gate_weight, up_held, up_weight, down_weight, blocks)
    hidden, kept = held(hidden), held(kept)
    came = [exchange(part, "hid", step + 1) for step, part in enumerate(sent)]
    parts = hid_sum([kept_part(hidden, kept, down_weight)] + came, blocks)
    return blk_sum(
        [parts[0]] + [exchange(parts[step], "blk", step) for step in range(1, blocks)]
    )


def solution(mesh):
    placed = (
        P(("blk", "regroup"), None),
        P(("blk", "regroup")),
        P(("blk", "regroup"), None),
        P(),
        P(None, ("blk", "hid")),
        P(None, ("blk", "hid")),
        P(("blk", "hid"), None),
    )
    return jax.shard_map(
        on_device,
        mesh=mesh,
        in_specs=placed,
        out_specs=P(("blk", "regroup"), "hid"),
        check_vma=False,
    )
```
